512 devices in a mesh: dp: 32 (over y, z_hi, x), tensor: 16 (over z_lo, core).
Axes of the slice: x: 4, y: 4, z: 16 (z_hi: 2, z_lo: 8; z = z_hi * 8 + z_lo), core: 2. Of those that a mesh axis runs over, the one named last changes fastest.
Arguments:
- context: bfloat16 [2048, 8192], P('tensor', 'dp'), may hold values from -6 to 6
- out_weight: bfloat16 [8192, 8192], P('dp', 'tensor'), may hold values from -0.125 to 0.125
- residual: bfloat16 [2048, 8192], P('dp', 'tensor'), may hold values from -6 to 6
- final_states: bfloat16 [2048, 8192], P('dp', 'tensor'), may hold values from -6 to 6
Outputs:
- gram: float32 [8192, 8192], P('dp', 'tensor')
- cross: float32 [8192, 8192], P('dp', 'tensor')
The draws below stay inside these ranges and needn't reach their ends.
All inputs are finite; a program needn't handle non-finite values.
Results may differ from the reference program's by a relative error of at most 0.0035.
Values may be sent and summed in bfloat16 or wider, within the bound.
A program may use at most 64 MiB of HBM per device.

```python
import jax
import jax.numpy as jnp
from jax import lax

D = 8192
TOK_DEV = 64
TOKENS = 2048
N_DP = 32


def with_spikes(array, stream_key, source, target, shards_of, factor):
    def block_of(dim):
        return (jnp.arange(array.shape[dim]) // (array.shape[dim] // shards_of)).reshape((-1,) + (1,) * (array.ndim - 1 - dim))

    one_side = jax.random.permutation(stream_key, shards_of)[block_of(target)]
    far = (block_of(target) + shards_of // 2) % shards_of
    return jnp.where((block_of(source) == one_side) | (block_of(source) == far), factor * array, array)


def block_levels(key, dims, pieces, smallest, high):
    gain, own = 1.0, jax.random.fold_in(key, 6)
    for position, shards_of in pieces:
        steps = jnp.exp(jax.random.uniform(jax.random.fold_in(own, position), (shards_of,), jnp.float32, smallest / len(pieces), high / len(pieces)))
        gain = gain * jnp.repeat(steps, dims[position] // shards_of).reshape([-1 if axis == position else 1 for axis in range(len(dims))])
    return gain


def scatter_about(key, extent, deviation, reach, shards=(), held_as=jnp.bfloat16):
    values = deviation * jax.random.normal(key, extent, jnp.float32)
    if shards:
        values = values * block_levels(key, extent, shards, -0.22, 0.18)
    return jnp.clip(values, -reach, reach).astype(held_as)


def bell_draw_with(stream_key, shape, width, bound, split, heavy, held_as=jnp.bfloat16):
    entries = width * jax.random.normal(stream_key, shape, jnp.float32)
    if split:
        entries = entries * block_levels(stream_key, shape, split, -0.22, 0.18)
    return jnp.clip(with_spikes(entries, jax.random.fold_in(stream_key, 3), *heavy), -bound, bound).astype(held_as)


def setup_inputs(seed: int = 0) -> dict:
    key_list = jax.random.split(jax.random.key(seed), 5)
    return {
        "context": scatter_about(key_list[0], (TOKENS, D), 1.0, 6.0, ((0, 16), (1, 32))),
        "out_weight": bell_draw_with(key_list[1], (D, D), D ** -0.5, 0.125, ((0, 32), (1, 16)), (0, 1, 32, 2.75)),
        "residual": scatter_about(key_list[2], (TOKENS, D), 1.0, 6.0, ((0, 32), (1, 16))),
        "final_states": scatter_about(key_list[3], (TOKENS, D), 1.0, 6.0, ((0, 32), (1, 16))),
    }


def reference(context, out_weight, residual, final_states):
    block = D // N_DP
    row_ids = lax.broadcasted_iota(jnp.int32, (TOKENS, 1), 0) // TOK_DEV

    def add_block(index, total):
        start = (index * block).astype(jnp.int32)
        columns = lax.dynamic_slice_in_dim(context, start, block, 1)
        weights = lax.dynamic_slice_in_dim(out_weight, start, block, 0)
        term = jnp.dot(columns, weights, preferred_element_type=jnp.float32)
        term = term + jnp.where(row_ids == index, residual.astype(jnp.float32), jnp.float32(0.0))
        return total + term

    summed = lax.fori_loop(0, N_DP, add_block, jnp.zeros((TOKENS, D), jnp.float32))
    states = summed.astype(jnp.bfloat16)
    gram = lax.dot_general(states, states, (((0,), (0,)), ((), ())), preferred_element_type=jnp.float32) / TOKENS
    cross = lax.dot_general(states, final_states, (((0,), (0,)), ((), ())), preferred_element_type=jnp.float32) / TOKENS
    return gram, cross
```

```python
import jax
import jax.numpy as jnp
from jax import lax
from jax.experimental import pallas as pl
from jax.experimental.pallas import tpu as pltpu
from jax.sharding import PartitionSpec as P

MESH = pl.DeviceIdType.MESH
OFFSETS = (0, -1, 1, -2)
LEVELS = (
    ((1, 0), (2, 0), (0, 1), (0, 2)),
    ((3, 0), (1, 1), (2, 1), (1, 2), (2, 2), (0, 3)),
    ((3, 1), (3, 2), (1, 3), (2, 3)),
    ((3, 3),),
)
ORDER = ((0, 0), (1, 0), (0, 1), (2, 0), (0, 2), (1, 1), (1, 2), (2, 1), (2, 2), (3, 0), (0, 3), (1, 3), (3, 1), (2, 3), (3, 2), (3, 3))


class Place:
    def __init__(self):
        d, t = lax.axis_index("dp"), lax.axis_index("tensor")
        self.y, self.zh, self.x = d // 8, (d // 4) % 2, d % 4
        self.zl, self.c = t // 2, t % 2
        self.q = self.y * 4 + self.x
        self.sg = 1 - 2 * self.c

    def at(self, y=None, zh=None, x=None, zl=None, c=None):
        y, zh, x, zl, c = (b if a is None else a for a, b in zip((y, zh, x, zl, c), (self.y, self.zh, self.x, self.zl, self.c)))
        return y * 8 + zh * 4 + x, zl * 2 + c


class Sends:
    def __init__(self):
        self.pending = []

    def start(self, src, dst, send_sem, recv_sem, device, cond=None):
        copy = pltpu.make_async_remote_copy(
            src_ref=src, dst_ref=dst, send_sem=send_sem, recv_sem=recv_sem, device_id=device, device_id_type=MESH
        )
        if cond is None:
            copy.start()
        else:
            pl.when(cond)(copy.start)
        self.pending.append((copy, cond))

    def drain(self):
        for copy, cond in self.pending:
            if cond is None:
                copy.wait_send()
            else:
                pl.when(cond)(copy.wait_send)
        self.pending = []


def arrived(ref, sem, device):
    pltpu.make_async_remote_copy(
        src_ref=ref, dst_ref=ref, send_sem=sem, recv_sem=sem, device_id=device, device_id_type=MESH
    ).wait_recv()


class Gather:
    def __init__(self, me, sends, own, slot, ssem, rsem):
        self.me, self.sends, self.own, self.slot, self.ssem, self.rsem = me, sends, own, slot, ssem, rsem

    def source(self, h, i, j):
        a, b = (i, j) if h == 0 else (j, i)
        return (self.me.x + self.me.sg * OFFSETS[a] + 8) % 4, (self.me.y + self.me.sg * OFFSETS[b] + 8) % 4

    def send(self, h, have, give, axis, sign):
        me = self.me
        px, py = self.source(h, *have)
        dst = self.slot(h, px, py)
        src = self.own(h) if have == (0, 0) else dst
        along_x = (axis == 0) == (h == 0)
        if along_x:
            device = me.at(x=(me.x + sign * me.sg + 4) % 4)
        else:
            device = me.at(y=(me.y + sign * me.sg + 4) % 4)
        k = h * 16 + give[0] * 4 + give[1]
        self.sends.start(src, dst, self.ssem.at[k], self.rsem.at[k], device)

    def begin(self, h):
        self.send(h, (0, 0), (1, 0), 0, 1)
        self.send(h, (0, 0), (2, 0), 0, -1)
        self.send(h, (0, 0), (0, 1), 1, 1)
        self.send(h, (0, 0), (0, 2), 1, -1)

    def event(self, h, i, j):
        px, py = self.source(h, i, j)
        arrived(self.slot(h, px, py), self.rsem.at[h * 16 + i * 4 + j], self.me.at(c=1 - self.me.c))
        if j == 0:
            if i == 1:
                self.send(h, (1, 0), (3, 0), 0, 1)
            self.send(h, (i, 0), (i, 1), 1, 1)
            self.send(h, (i, 0), (i, 2), 1, -1)
        elif j == 1:
            self.send(h, (i, 1), (i, 3), 1, 1)

    def level(self, n):
        for i, j in LEVELS[n]:
            for h in (0, 1):
                self.event(h, i, j)


def kernel(
    ctx, w, res, fin, gram, cross,
    wbuf, cbuf, rbuf, part, other, fbuf, sbuf, lbuf,
    w_s, w_r, f_s, f_r, s_s, s_r, a_s, a_r, z_s, z_r, b_s, b_r, e_s, e_r, x_s, x_r, l_s, l_r, own_sem,
):
    me = Place()
    sends = Sends()
    sibling = me.at(c=1 - me.c)
    partner = me.at(zh=1 - me.zh)

    barrier = pltpu.get_barrier_semaphore()

    def greet(device):
        pl.semaphore_signal(barrier, inc=1, device_id=device, device_id_type=MESH)

    for k in range(1, 16):
        p = (me.q + k) % 16
        greet(me.at(y=p // 4, x=p % 4))
    for k in range(16):
        greet(me.at(y=k // 4, x=k % 4, c=1 - me.c))
    for k in range(1, 8):
        greet(me.at(zl=(me.zl + k) % 8))
    greet(partner)
    pl.semaphore_wait(barrier, 15 + 16 + 7 + 1)

    slot_of = lambda zl: (zl % 2) * 4 + zl // 2
    lanes = pl.ds(pl.multiple_of(me.q * 256, 256), 256)
    for i in range(8):
        p = 8 * me.c + i
        src, dst = ctx.at[pl.ds(16 * i, 16)], cbuf.at[slot_of(me.zl), :, lanes]
        k = me.q % 8
        mine = (p == me.q) & (me.q // 8 == me.c)
        sends.start(src, dst, a_s.at[i], a_r.at[k], me.at(y=p // 4, x=p % 4, c=me.q // 8), cond=jnp.logical_not(mine))
        pl.when(mine)(pltpu.make_async_copy(src, dst, a_r.at[k]).start)

    gather_w = Gather(
        me, sends,
        lambda h: w.at[pl.ds(128 * h, 128)],
        lambda h, px, py: wbuf.at[py * 4 + px, pl.ds(128 * h, 128)],
        w_s, w_r,
    )
    gather_w.begin(0)
    gather_w.begin(1)
    own_w = pltpu.make_async_copy(w, wbuf.at[me.q], own_sem.at[0])
    own_w.start()

    own_f = pltpu.make_async_copy(fin, fbuf.at[me.zh, me.y, pl.ds(4 * me.x, 4)], own_sem.at[1])
    own_f.start()
    sends.start(fin, fbuf.at[me.zh, me.y, pl.ds(4 * me.x, 4)], x_s.at[0], x_r.at[0], partner)

    for j in range(4):
        mine = (me.x == me.y) & (me.x == j)
        sends.start(res.at[j], rbuf.at[me.y], e_s.at[j], e_r.at[me.y], me.at(y=me.x, x=j), cond=jnp.logical_not(mine))
        pl.when(mine)(pltpu.make_async_copy(res.at[j], rbuf.at[me.y], e_r.at[me.y]).start)

    half = pl.ds(pl.multiple_of(me.c * 2048, 2048), 2048)
    other_half = pl.ds(pl.multiple_of((1 - me.c) * 2048, 2048), 2048)
    for i in range(8):
        piece = cbuf.at[slot_of(me.zl), :, pl.ds(pl.multiple_of((me.c * 8 + i) * 256, 256), 256)]
        arrived(piece, a_r.at[i], sibling)
    piece = cbuf.at[slot_of(me.zl), :, half]
    for k in range(1, 8):
        sends.start(piece, piece, z_s.at[k], z_r.at[k], me.at(zl=(me.zl + k) % 8))
    sends.start(piece, piece, b_s.at[0], b_r.at[0], sibling)

    def along_z(k):
        piece = cbuf.at[slot_of((me.zl - k + 8) % 8), :, half]
        arrived(piece, z_r.at[k], sibling)
        sends.start(piece, piece, b_s.at[k], b_r.at[k], sibling)

    gather_w.level(0)
    along_z(1)
    along_z(7)
    gather_w.level(1)
    for k in (2, 6, 3, 5, 4):
        along_z(k)
    gather_w.level(2)
    gather_w.level(3)
    for k in range(8):
        arrived(cbuf.at[slot_of((me.zl - k + 8) % 8), :, other_half], b_r.at[k], sibling)
    own_w.wait()

    part[...] = jnp.zeros_like(part)

    def project(k, carry):
        cols = pl.ds(pl.multiple_of(k * 512, 512), 512)
        a = cbuf[:, :, cols].reshape(128, 512)
        b = wbuf[pl.ds(2 * k, 2)].reshape(512, 512)
        part[...] += jnp.dot(a, b, preferred_element_type=jnp.float32).reshape(8, 16, 512)
        return carry

    lax.fori_loop(0, 8, project, 0)
    for j in range(4):
        arrived(rbuf.at[j], e_r.at[j], sibling)
    mine = pl.ds(4 * me.zh, 4)
    part[mine] = part[mine] + rbuf[...].astype(jnp.float32)
    sends.start(part, other, x_s.at[1], x_r.at[1], partner)

    own_f.wait()
    fslot = lambda h, px, py: fbuf.at[h, py, pl.ds(4 * px, 4)]
    arrived(fbuf.at[1 - me.zh, me.y, pl.ds(4 * me.x, 4)], x_r.at[0], sibling)
    gather_f = Gather(me, sends, lambda h: fslot(h, me.x, me.y), fslot, f_s, f_r)
    gather_f.begin(0)
    gather_f.begin(1)
    for n in range(4):
        gather_f.level(n)

    arrived(other, x_r.at[1], sibling)
    sbuf[:, me.q] = (part[...] + other[...]).astype(jnp.bfloat16)
    sslot = lambda h, px, py: sbuf.at[pl.ds(4 * h, 4), py * 4 + px]
    gather_s = Gather(me, sends, lambda h: sslot(h, me.x, me.y), sslot, s_s, s_r)
    gather_s.begin(0)
    gather_s.begin(1)

    lead = me.x // 2
    on_line = me.c == lead
    root = 2 * me.y + me.zh
    is_root = on_line & (me.zl == root)
    fed = on_line & (me.zl != root)
    lsg = 1 - 2 * lead
    lcols = pl.ds(pl.multiple_of((me.x % 2) * 256, 256), 256)
    above, below = me.zl > root, me.zl < root
    up_hop, down_hop = (8 - root) // 2, (root + 1) // 2
    o_up, o_down = me.zl - root, root - me.zl
    has_up = on_line & (
        ((me.zl == root) & (root < 7))
        | (above & (o_up >= up_hop) & (me.zl < 7))
        | (below & (o_down <= down_hop) & (o_down > 1))
    )
    has_down = on_line & (
        ((me.zl == root) & (root > 0))
        | (below & (o_down >= down_hop) & (me.zl > 0))
        | (above & (o_up <= up_hop) & (o_up > 1))
    )
    at_root = jnp.where(me.zl == root, 1, 0)
    up_zl = jnp.minimum(me.zl + at_root * up_hop + (1 - at_root), 7)
    down_zl = jnp.maximum(me.zl - at_root * down_hop - (1 - at_root), 0)

    def place_of(m):
        a, b = ORDER[m]
        px, py = (me.x + lsg * OFFSETS[a] + 8) % 4, (me.y + lsg * OFFSETS[b] + 8) % 4
        return py * 4 + px

    def pass_on(m, who):
        piece = lbuf.at[:, place_of(m)]
        sends.start(piece, piece, l_s.at[m], l_r.at[m], me.at(zl=up_zl), cond=has_up & who)
        sends.start(piece, piece, l_s.at[16 + m], l_r.at[m], me.at(zl=down_zl), cond=has_down & who)
        sends.start(piece, piece, l_s.at[32 + m], l_r.at[16 + m], sibling, cond=who)

    def root_sends(m):
        place = place_of(m)

        @pl.when(is_root)
        def _():
            lbuf[:, place] = sbuf[:, place, :, lcols]

        pass_on(m, is_root)

    def take(m):
        piece = lbuf.at[:, place_of(m)]
        pl.when(fed)(lambda: arrived(piece, l_r.at[m], sibling))
        pass_on(m, fed)
        pl.when(jnp.logical_not(on_line))(lambda: arrived(piece, l_r.at[16 + m], sibling))

    root_sends(0)
    gather_s.level(0)
    for m in range(1, 5):
        root_sends(m)
    gather_s.level(1)
    for m in range(5, 11):
        root_sends(m)
    gather_s.level(2)
    for m in range(11, 15):
        root_sends(m)
    for m in range(8):
        take(m)
    gather_s.level(3)
    root_sends(15)

    gram[...] = jnp.zeros_like(gram)
    cross[...] = jnp.zeros_like(cross)

    def add(m):
        place = place_of(m)
        a = lbuf[:, place].reshape(128, 256)
        s = sbuf[:, place].reshape(128, 512)
        f = fbuf[:, :, place].reshape(128, 512)
        dims = (((0,), (0,)), ((), ()))
        gram[...] += lax.dot_general(a, s, dims, preferred_element_type=jnp.float32)
        cross[...] += lax.dot_general(a, f, dims, preferred_element_type=jnp.float32)

    for m in range(8, 16):
        take(m)
        add(2 * (m - 8))
        add(2 * (m - 8) + 1)
    gram[...] = gram[...] * (1.0 / 2048)
    cross[...] = cross[...] * (1.0 / 2048)
    sends.drain()


def body(context, out_weight, residual, final_states):
    vmem = pl.BlockSpec(memory_space=pltpu.VMEM)
    dma = lambda n: pltpu.SemaphoreType.DMA((n,))
    bf16, f32 = jnp.bfloat16, jnp.float32
    out = jax.ShapeDtypeStruct((256, 512), f32)
    return pl.pallas_call(
        kernel,
        out_shape=(out, out),
        in_specs=[vmem] * 4,
        out_specs=(vmem, vmem),
        scratch_shapes=[
            pltpu.VMEM((16, 256, 512), bf16),
            pltpu.VMEM((8, 16, 4096), bf16),
            pltpu.VMEM((4, 16, 512), bf16),
            pltpu.VMEM((8, 16, 512), f32),
            pltpu.VMEM((8, 16, 512), f32),
            pltpu.VMEM((2, 4, 16, 16, 512), bf16),
            pltpu.VMEM((8, 16, 16, 512), bf16),
            pltpu.VMEM((8, 16, 16, 256), bf16),
            dma(32), dma(32), dma(32), dma(32), dma(32), dma(32),
            dma(8), dma(8), dma(8), dma(8), dma(8), dma(8),
            dma(4), dma(4), dma(2), dma(2), dma(48), dma(32), dma(2),
        ],
        compiler_params=pltpu.CompilerParams(collective_id=0, has_side_effects=True, vmem_limit_bytes=40 << 20),
        cost_estimate=pl.CostEstimate(flops=1 << 31, bytes_accessed=1 << 21, transcendentals=0),
    )(context, out_weight, residual.reshape(4, 16, 512), final_states.reshape(4, 16, 512))


def solution(mesh):
    in_specs = (P("tensor", "dp"), P("dp", "tensor"), P("dp", "tensor"), P("dp", "tensor"))
    out_specs = (P("dp", "tensor"), P("dp", "tensor"))
    return jax.shard_map(body, mesh=mesh, in_specs=in_specs, out_specs=out_specs, check_vma=False)
```

```python
import jax
import jax.numpy as jnp
from jax import lax
from jax.experimental import pallas as pl
from jax.experimental.pallas import tpu as pltpu
from jax.sharding import PartitionSpec as P

MESH = pl.DeviceIdType.MESH
OFFSETS = (0, -1, 1, -2)
LEVELS = (
    ((1, 0), (2, 0), (0, 1), (0, 2)),
    ((3, 0), (1, 1), (2, 1), (1, 2), (2, 2), (0, 3)),
    ((3, 1), (3, 2), (1, 3), (2, 3)),
    ((3, 3),),
)
class Place:
    def __init__(self):
        d, t = lax.axis_index("dp"), lax.axis_index("tensor")
        self.y, self.zh, self.x = d // 8, (d // 4) % 2, d % 4
        self.zl, self.c = t // 2, t % 2
        self.q = self.y * 4 + self.x
        self.n = self.x * 4 + self.y
        self.sg = 1 - 2 * self.c

    def at(self, y=None, zh=None, x=None, zl=None, c=None):
        y, zh, x, zl, c = (b if a is None else a for a, b in zip((y, zh, x, zl, c), (self.y, self.zh, self.x, self.zl, self.c)))
        return y * 8 + zh * 4 + x, zl * 2 + c


class Sends:
    def __init__(self):
        self.pending = []

    def start(self, src, dst, send_sem, recv_sem, device, cond=None):
        copy = pltpu.make_async_remote_copy(
            src_ref=src, dst_ref=dst, send_sem=send_sem, recv_sem=recv_sem, device_id=device, device_id_type=MESH
        )
        if cond is None:
            copy.start()
        else:
            pl.when(cond)(copy.start)
        self.pending.append((copy, cond))

    def drain(self):
        for copy, cond in self.pending:
            if cond is None:
                copy.wait_send()
            else:
                pl.when(cond)(copy.wait_send)
        self.pending = []


def arrived(ref, sem, device):
    pltpu.make_async_remote_copy(
        src_ref=ref, dst_ref=ref, send_sem=sem, recv_sem=sem, device_id=device, device_id_type=MESH
    ).wait_recv()


class Gather:
    def __init__(self, me, sends, own, slot, ssem, rsem):
        self.me, self.sends, self.own, self.slot, self.ssem, self.rsem = me, sends, own, slot, ssem, rsem

    def source(self, h, i, j):
        a, b = (i, j) if h == 0 else (j, i)
        return (self.me.x + self.me.sg * OFFSETS[a] + 8) % 4, (self.me.y + self.me.sg * OFFSETS[b] + 8) % 4

    def send(self, h, have, give, axis, sign):
        me = self.me
        px, py = self.source(h, *have)
        dst = self.slot(h, px, py)
        src = self.own(h) if have == (0, 0) else dst
        along_x = (axis == 0) == (h == 0)
        if along_x:
            device = me.at(x=(me.x + sign * me.sg + 4) % 4)
        else:
            device = me.at(y=(me.y + sign * me.sg + 4) % 4)
        k = h * 16 + give[0] * 4 + give[1]
        self.sends.start(src, dst, self.ssem.at[k], self.rsem.at[k], device)

    def begin(self, h):
        self.send(h, (0, 0), (1, 0), 0, 1)
        self.send(h, (0, 0), (2, 0), 0, -1)
        self.send(h, (0, 0), (0, 1), 1, 1)
        self.send(h, (0, 0), (0, 2), 1, -1)

    def event(self, h, i, j):
        px, py = self.source(h, i, j)
        arrived(self.slot(h, px, py), self.rsem.at[h * 16 + i * 4 + j], self.me.at(c=1 - self.me.c))
        if j == 0:
            if i == 1:
                self.send(h, (1, 0), (3, 0), 0, 1)
            self.send(h, (i, 0), (i, 1), 1, 1)
            self.send(h, (i, 0), (i, 2), 1, -1)
        elif j == 1:
            self.send(h, (i, 1), (i, 3), 1, 1)

    def level(self, n):
        for i, j in LEVELS[n]:
            for h in (0, 1):
                self.event(h, i, j)


def kernel(
    ctx, w, res, fin, gram, cross,
    wbuf, cbuf, rbuf, part, mine_out, other, fbuf, sbuf, lbuf,
    w_s, w_r, f_s, f_r, s_s, s_r, a_s, a_r, z_s, z_r, b_s, b_r, e_s, e_r, x_s, x_r, t_s, t_r, l_s, l_r, own_sem,
):
    me = Place()
    sends = Sends()
    sibling = me.at(c=1 - me.c)
    partner = me.at(zh=1 - me.zh)
    lead = me.x // 2
    root = 2 * me.y + me.zh
    on_line = me.c == lead
    is_root = on_line & (me.zl == root)
    feeds = me.zl % 2 == me.zh
    other_core = 1 - me.c
    to_core, from_core = me.q // 8, me.x // 2
    swaps_self = (me.x // 2 == me.c) & (me.q // 8 == me.c)

    own_w = pltpu.make_async_copy(w, wbuf.at[me.q], own_sem.at[0])
    own_w.start()
    own_f = pltpu.make_async_copy(fin, fbuf.at[me.zh, me.y, pl.ds(4 * me.x, 4)], own_sem.at[1])
    own_f.start()

    barrier = pltpu.get_barrier_semaphore()

    def greet(device, cond=None):
        signal = lambda: pl.semaphore_signal(barrier, inc=1, device_id=device, device_id_type=MESH)
        if cond is None:
            signal()
        else:
            pl.when(cond)(signal)

    for k in (1, 2, 3):
        greet(me.at(y=(me.y + k) % 4))
    for k in (1, 3):
        greet(me.at(x=(me.x + k) % 4))
    for k in range(1, 8):
        greet(me.at(zl=(me.zl + k) % 8))
    greet(partner)
    greet(sibling)
    for i in range(8):
        p = 8 * me.c + i
        greet(me.at(y=p // 4, x=p % 4, c=from_core), jnp.logical_not((p == me.q) & (from_core == me.c)))

    @pl.when(is_root)
    def _():
        for k in range(1, 16):
            p = (me.q + k) % 16
            greet(me.at(y=p // 4, x=p % 4))

    here = feeds & (me.y == me.zl // 2) & (me.x // 2 == me.c)
    count = 3 + 2 + 7 + 1 + 1 + 8 - jnp.where(swaps_self, 1, 0) + jnp.where(feeds, 2, 0) - jnp.where(here, 1, 0)
    pl.semaphore_wait(barrier, count)

    slot_of = lambda zl: (zl % 2) * 4 + zl // 2
    lanes = pl.ds(pl.multiple_of(me.q * 256, 256), 256)
    for i in range(8):
        px, py = 2 * me.c + i // 4, i % 4
        src, dst = ctx.at[pl.ds(16 * i, 16)], cbuf.at[slot_of(me.zl), :, lanes]
        k = me.q % 8
        mine = (px == me.x) & (py == me.y) & (to_core == me.c)
        sends.start(src, dst, a_s.at[i], a_r.at[k], me.at(y=py, x=px, c=to_core), cond=jnp.logical_not(mine))
        pl.when(mine)(pltpu.make_async_copy(src, dst, a_r.at[k]).start)

    gather_w = Gather(
        me, sends,
        lambda h: w.at[pl.ds(128 * h, 128)],
        lambda h, px, py: wbuf.at[py * 4 + px, pl.ds(128 * h, 128)],
        w_s, w_r,
    )
    gather_w.begin(0)
    gather_w.begin(1)
    sends.start(fin, fbuf.at[me.zh, me.y, pl.ds(4 * me.x, 4)], x_s.at[0], x_r.at[0], partner)

    for k in range(4):
        j = (me.y + k) % 4
        if k == 0:
            pltpu.make_async_copy(res.at[j], rbuf.at[me.y], e_r.at[0]).start()
        else:
            sends.start(res.at[j], rbuf.at[me.y], e_s.at[k], e_r.at[k], me.at(y=j))

    half = pl.ds(pl.multiple_of(me.c * 2048, 2048), 2048)
    other_half = pl.ds(pl.multiple_of(other_core * 2048, 2048), 2048)
    for i in range(8):
        piece = cbuf.at[slot_of(me.zl), :, pl.ds(pl.multiple_of((me.c * 8 + i) * 256, 256), 256)]
        arrived(piece, a_r.at[i], sibling)

    base, pos = (me.zl // 4) * 4, me.zl % 4
    far = (me.zl + 4) % 8
    line = lambda zl: cbuf.at[slot_of(zl), :, half]
    sends.start(line(me.zl), line(me.zl), z_s.at[4], z_r.at[4], me.at(zl=far))
    for k in (1, 2, 3):
        sends.start(line(me.zl), line(me.zl), z_s.at[k], z_r.at[k], me.at(zl=base + (pos + k) % 4))
    sends.start(line(me.zl), line(me.zl), b_s.at[0], b_r.at[0], sibling)

    def from_z(k):
        zl = far if k == 4 else base + (pos - k) % 4 if k < 4 else (4 - base) + (pos - (k - 4)) % 4
        return zl

    def along_z(k):
        piece = line(from_z(k))
        arrived(piece, z_r.at[k], sibling)
        if k == 4:
            for i in (1, 2, 3):
                sends.start(piece, piece, z_s.at[4 + i], z_r.at[4 + i], me.at(zl=base + (pos + i) % 4))
        sends.start(piece, piece, b_s.at[k], b_r.at[k], sibling)

    gather_w.level(0)
    along_z(4)
    along_z(1)
    along_z(3)
    along_z(2)
    gather_w.level(1)
    for k in (5, 7, 6):
        along_z(k)
    gather_w.level(2)
    arrived(fbuf.at[1 - me.zh, me.y, pl.ds(4 * me.x, 4)], x_r.at[0], sibling)
    own_f.wait()
    fslot = lambda h, px, py: fbuf.at[(me.zh + h) % 2, py, pl.ds(4 * px, 4)]
    gather_f = Gather(me, sends, lambda h: fslot(h, me.x, me.y), fslot, f_s, f_r)
    gather_f.begin(0)
    gather_f.begin(1)
    gather_w.level(3)
    for k in range(8):
        zl = me.zl if k == 0 else from_z(k)
        arrived(cbuf.at[slot_of(zl), :, other_half], b_r.at[k], sibling)
    own_w.wait()

    part[...] = jnp.zeros_like(part)

    def project(k, carry):
        cols = pl.ds(pl.multiple_of(k * 512, 512), 512)
        a = cbuf[:, :, cols].reshape(128, 512)
        b = wbuf[pl.ds(2 * k, 2)].reshape(512, 512)
        part[...] += jnp.dot(a, b, preferred_element_type=jnp.float32).reshape(8, 16, 512)
        return carry

    lax.fori_loop(0, 8, project, 0)
    for k in range(4):
        arrived(rbuf.at[(me.y - k) % 4], e_r.at[k], sibling)
    mine = pl.ds(4 * me.zh, 4)
    part[mine] = part[mine] + rbuf[...].astype(jnp.float32)
    mine_out[...] = part[...].astype(jnp.bfloat16)
    for h in (0, 1):
        rows = pl.ds(4 * h, 4)
        sends.start(mine_out.at[rows], other.at[rows], x_s.at[1 + h], x_r.at[1 + h], partner)
    for n in range(4):
        gather_f.level(n)

    sslot = lambda h, px, py: sbuf.at[pl.ds(4 * h, 4), px * 4 + py]
    gather_s = Gather(me, sends, lambda h: sslot(h, me.x, me.y), sslot, s_s, s_r)
    for h in (0, 1):
        rows = pl.ds(4 * h, 4)
        arrived(other.at[rows], x_r.at[1 + h], sibling)
        sbuf[rows, me.n] = (part[rows] + other[rows].astype(jnp.float32)).astype(jnp.bfloat16)
        for j in (0, 1):
            px = 2 * me.c + j
            self_here = feeds & (me.y == me.zl // 2) & (me.x == px)
            src, dst = sbuf.at[rows, me.n, :, pl.ds(256 * j, 256)], lbuf.at[rows, me.n]
            sem = t_r.at[h * 16 + me.n]
            sends.start(
                src, dst, t_s.at[h * 2 + j], sem, me.at(y=me.zl // 2, x=px), cond=feeds & jnp.logical_not(self_here)
            )
            pl.when(self_here)(pltpu.make_async_copy(src, dst, sem).start)
        gather_s.begin(h)

    fed = on_line & (me.zl != root)
    above, below = me.zl > root, me.zl < root
    up_hop, down_hop = (8 - root) // 2, (root + 1) // 2
    o_up, o_down = me.zl - root, root - me.zl
    has_up = on_line & (
        ((me.zl == root) & (root < 7))
        | (above & (o_up >= up_hop) & (me.zl < 7))
        | (below & (o_down <= down_hop) & (o_down > 1))
    )
    has_down = on_line & (
        ((me.zl == root) & (root > 0))
        | (below & (o_down >= down_hop) & (me.zl > 0))
        | (above & (o_up <= up_hop) & (o_up > 1))
    )
    at_root = jnp.where(me.zl == root, 1, 0)
    up_zl = jnp.minimum(me.zl + at_root * up_hop + (1 - at_root), 7)
    down_zl = jnp.maximum(me.zl - at_root * down_hop - (1 - at_root), 0)

    def message(m):
        return lbuf.at[pl.ds(4 * (m // 8), 4), pl.ds(2 * (m % 8), 2)]

    def pass_on(m, who):
        piece = message(m)
        sends.start(piece, piece, l_s.at[m], l_r.at[m], me.at(zl=up_zl), cond=has_up & who)
        sends.start(piece, piece, l_s.at[16 + m], l_r.at[m], me.at(zl=down_zl), cond=has_down & who)
        sends.start(piece, piece, l_s.at[32 + m], l_r.at[16 + m], sibling, cond=who)

    def root_sends(m):
        h, g = m // 8, m % 8

        @pl.when(is_root)
        def _():
            for n in (2 * g, 2 * g + 1):
                arrived(lbuf.at[pl.ds(4 * h, 4), n], t_r.at[h * 16 + n], sibling)

        pass_on(m, is_root)

    def take(m):
        pl.when(fed)(lambda: arrived(message(m), l_r.at[m], sibling))
        pass_on(m, fed)
        pl.when(jnp.logical_not(on_line))(lambda: arrived(message(m), l_r.at[16 + m], sibling))

    gather_s.level(0)
    for m in range(8):
        root_sends(m)
    gather_s.level(1)
    for m in range(8, 16):
        root_sends(m)
    for m in range(8):
        take(m)
    gather_s.level(2)
    gather_s.level(3)

    gram[...] = jnp.zeros_like(gram)
    cross[...] = jnp.zeros_like(cross)

    def add(g):
        pair = pl.ds(2 * g, 2)
        a = lbuf[:, pair].reshape(256, 256)
        s = sbuf[:, pair].reshape(256, 512)
        f = fbuf[:, :, pair].reshape(256, 512)
        dims = (((0,), (0,)), ((), ()))
        gram[...] += lax.dot_general(a, s, dims, preferred_element_type=jnp.float32)
        cross[...] += lax.dot_general(a, f, dims, preferred_element_type=jnp.float32)

    for g in range(8):
        take(8 + g)
        add(g)
    gram[...] = gram[...] * (1.0 / 2048)
    cross[...] = cross[...] * (1.0 / 2048)
    sends.drain()


def body(context, out_weight, residual, final_states):
    vmem, hbm = pl.BlockSpec(memory_space=pltpu.VMEM), pl.BlockSpec(memory_space=pl.ANY)
    dma = lambda n: pltpu.SemaphoreType.DMA((n,))
    bf16, f32 = jnp.bfloat16, jnp.float32
    out = jax.ShapeDtypeStruct((256, 512), f32)
    return pl.pallas_call(
        kernel,
        out_shape=(out, out),
        in_specs=[hbm] * 4,
        out_specs=(vmem, vmem),
        scratch_shapes=[
            pltpu.VMEM((16, 256, 512), bf16),
            pltpu.VMEM((8, 16, 4096), bf16),
            pltpu.VMEM((4, 16, 512), bf16),
            pltpu.VMEM((8, 16, 512), f32),
            pltpu.VMEM((8, 16, 512), bf16),
            pltpu.VMEM((8, 16, 512), bf16),
            pltpu.VMEM((2, 4, 16, 16, 512), bf16),
            pltpu.VMEM((8, 16, 16, 512), bf16),
            pltpu.VMEM((8, 16, 16, 256), bf16),
            dma(32), dma(32), dma(32), dma(32), dma(32), dma(32),
            dma(8), dma(8), dma(8), dma(8), dma(8), dma(8),
            dma(4), dma(4), dma(3), dma(3), dma(4), dma(32), dma(48), dma(32), dma(2),
        ],
        compiler_params=pltpu.CompilerParams(collective_id=0, has_side_effects=True, vmem_limit_bytes=56 << 20),
        cost_estimate=pl.CostEstimate(flops=1 << 31, bytes_accessed=1 << 21, transcendentals=0),
    )(context, out_weight, residual.reshape(4, 16, 512), final_states.reshape(4, 16, 512))


def solution(mesh):
    in_specs = (P("tensor", "dp"), P("dp", "tensor"), P("dp", "tensor"), P("dp", "tensor"))
    out_specs = (P("dp", "tensor"), P("dp", "tensor"))
    return jax.shard_map(body, mesh=mesh, in_specs=in_specs, out_specs=out_specs, check_vma=False)
```

```python
import jax
import jax.numpy as jnp
from jax import lax
from jax.experimental import pallas as pl
from jax.experimental.pallas import tpu as pltpu
from jax.sharding import PartitionSpec as P

MESH = pl.DeviceIdType.MESH
OFFSETS = (0, -1, 1, -2)
LEVELS = (((1, 0), (2, 0), (0, 1)), ((3, 0), (1, 1), (2, 1)), ((3, 1),))
LAST = ((0, 2), (1, 2), (2, 2), (0, 3), (3, 2), (1, 3), (2, 3), (3, 3))
EARLY = ((0, 0), (1, 0), (0, 1), (2, 0), (0, 2), (1, 1), (1, 2), (2, 1), (2, 2), (3, 0), (0, 3))
LATE = ((3, 1), (1, 3), (3, 2), (2, 3), (3, 3))


class Place:
    def __init__(self):
        d, t = lax.axis_index("dp"), lax.axis_index("tensor")
        self.y, self.zh, self.x = d // 8, (d // 4) % 2, d % 4
        self.zl, self.c = t // 2, t % 2
        self.q = self.y * 4 + self.x
        self.n = self.x * 4 + self.y
        self.sg = 1 - 2 * self.c

    def at(self, y=None, zh=None, x=None, zl=None, c=None):
        y, zh, x, zl, c = (b if a is None else a for a, b in zip((y, zh, x, zl, c), (self.y, self.zh, self.x, self.zl, self.c)))
        return y * 8 + zh * 4 + x, zl * 2 + c


class Sends:
    def __init__(self):
        self.pending = []

    def start(self, src, dst, send_sem, recv_sem, device, cond=None):
        copy = pltpu.make_async_remote_copy(
            src_ref=src, dst_ref=dst, send_sem=send_sem, recv_sem=recv_sem, device_id=device, device_id_type=MESH
        )
        if cond is None:
            copy.start()
        else:
            pl.when(cond)(copy.start)
        self.pending.append((copy, cond))

    def drain(self):
        for copy, cond in self.pending:
            if cond is None:
                copy.wait_send()
            else:
                pl.when(cond)(copy.wait_send)
        self.pending = []


def arrived(ref, sem, device):
    pltpu.make_async_remote_copy(
        src_ref=ref, dst_ref=ref, send_sem=sem, recv_sem=sem, device_id=device, device_id_type=MESH
    ).wait_recv()


class Gather:
    def __init__(self, me, sends, own, slot, ssem, rsem):
        self.me, self.sends, self.own, self.slot, self.ssem, self.rsem = me, sends, own, slot, ssem, rsem

    def source(self, h, i, j):
        a, b = (i, j) if h % 2 == 0 else (j, i)
        return (self.me.x + self.me.sg * OFFSETS[a] + 8) % 4, (self.me.y + self.me.sg * OFFSETS[b] + 8) % 4

    def send(self, h, have, give, axis, sign):
        me = self.me
        px, py = self.source(h, *have)
        dst = self.slot(h, px, py)
        src = self.own(h) if have == (0, 0) else dst
        along_x = (axis == 0) == (h % 2 == 0)
        if along_x:
            device = me.at(x=(me.x + sign * me.sg + 4) % 4)
        else:
            device = me.at(y=(me.y + sign * me.sg + 4) % 4)
        k = h * 16 + give[0] * 4 + give[1]
        self.sends.start(src, dst, self.ssem.at[k], self.rsem.at[k], device)

    def begin(self, h):
        self.send(h, (0, 0), (1, 0), 0, 1)
        self.send(h, (0, 0), (2, 0), 0, -1)
        self.send(h, (0, 0), (0, 1), 1, 1)
        self.send(h, (0, 0), (0, 2), 1, -1)

    def event(self, h, i, j):
        px, py = self.source(h, i, j)
        arrived(self.slot(h, px, py), self.rsem.at[h * 16 + i * 4 + j], self.me.at(c=1 - self.me.c))
        if j == 0:
            if i == 1:
                self.send(h, (1, 0), (3, 0), 0, 1)
            self.send(h, (i, 0), (i, 1), 1, 1)
            self.send(h, (i, 0), (i, 2), 1, -1)
        elif j == 1:
            self.send(h, (i, 1), (i, 3), 1, 1)

    def level(self, n, parts=(0, 1)):
        for i, j in LEVELS[n]:
            for h in parts:
                self.event(h, i, j)

    def finish(self, parts=(0, 1), which=LAST):
        for i, j in which:
            for h in parts:
                self.event(h, i, j)


def kernel(
    ctx, w, res, fin, gram, cross,
    wbuf, cbuf, rbuf, part, mine_out, other, fbuf, sbuf, lbuf,
    w_s, w_r, f_s, f_r, s_s, s_r, a_s, a_r, z_s, z_r, b_s, b_r, e_s, e_r, x_s, x_r, t_s, t_r, l_s, l_r, own_sem,
):
    me = Place()
    sends = Sends()
    sibling = me.at(c=1 - me.c)
    partner = me.at(zh=1 - me.zh)
    lead = me.x // 2
    root = 2 * me.y + me.zh
    on_line = me.c == lead
    is_root = on_line & (me.zl == root)
    feeds = me.zl % 2 == me.zh
    other_core = 1 - me.c
    to_core, from_core = me.q // 8, me.x // 2
    swaps_self = (me.x // 2 == me.c) & (me.q // 8 == me.c)

    own_w = pltpu.make_async_copy(w, wbuf.at[me.q], own_sem.at[0])
    own_w.start()
    own_f = pltpu.make_async_copy(fin, fbuf.at[me.zh, me.y, pl.ds(4 * me.x, 4)], own_sem.at[1])
    own_f.start()

    barrier = pltpu.get_barrier_semaphore()

    def greet(device, cond=None):
        signal = lambda: pl.semaphore_signal(barrier, inc=1, device_id=device, device_id_type=MESH)
        if cond is None:
            signal()
        else:
            pl.when(cond)(signal)

    for k in (1, 2, 3):
        greet(me.at(y=(me.y + k) % 4))
    for k in (1, 3):
        greet(me.at(x=(me.x + k) % 4))
    for k in range(1, 8):
        greet(me.at(zl=(me.zl + k) % 8))
    greet(partner)
    greet(sibling)
    for i in range(8):
        p = 8 * me.c + i
        greet(me.at(y=p // 4, x=p % 4, c=from_core), jnp.logical_not((p == me.q) & (from_core == me.c)))

    @pl.when(is_root)
    def _():
        for k in range(1, 16):
            p = (me.q + k) % 16
            greet(me.at(y=p // 4, x=p % 4))

    here = feeds & (me.y == me.zl // 2) & (me.x // 2 == me.c)
    count = 3 + 2 + 7 + 1 + 1 + 8 - jnp.where(swaps_self, 1, 0) + jnp.where(feeds, 2, 0) - jnp.where(here, 1, 0)
    pl.semaphore_wait(barrier, count)

    slot_of = lambda zl: (zl % 2) * 4 + zl // 2
    lanes = pl.ds(pl.multiple_of(me.q * 256, 256), 256)
    for i in range(8):
        px, py = 2 * me.c + i // 4, i % 4
        src, dst = ctx.at[pl.ds(16 * i, 16)], cbuf.at[slot_of(me.zl), :, lanes]
        k = me.q % 8
        mine = (px == me.x) & (py == me.y) & (to_core == me.c)
        sends.start(src, dst, a_s.at[i], a_r.at[k], me.at(y=py, x=px, c=to_core), cond=jnp.logical_not(mine))
        pl.when(mine)(pltpu.make_async_copy(src, dst, a_r.at[k]).start)

    gather_w = Gather(
        me, sends,
        lambda h: w.at[pl.ds(128 * h, 128)],
        lambda h, px, py: wbuf.at[py * 4 + px, pl.ds(128 * h, 128)],
        w_s, w_r,
    )
    gather_w.begin(0)
    gather_w.begin(1)
    sends.start(fin, fbuf.at[me.zh, me.y, pl.ds(4 * me.x, 4)], x_s.at[0], x_r.at[0], partner)

    for k in range(4):
        j = (me.y + k) % 4
        if k == 0:
            pltpu.make_async_copy(res.at[j], rbuf.at[me.y], e_r.at[0]).start()
        else:
            sends.start(res.at[j], rbuf.at[me.y], e_s.at[k], e_r.at[k], me.at(y=j))

    half = pl.ds(pl.multiple_of(me.c * 2048, 2048), 2048)
    other_half = pl.ds(pl.multiple_of(other_core * 2048, 2048), 2048)
    gather_w.level(0)
    for i in range(8):
        piece = cbuf.at[slot_of(me.zl), :, pl.ds(pl.multiple_of((me.c * 8 + i) * 256, 256), 256)]
        arrived(piece, a_r.at[i], sibling)

    base, pos = (me.zl // 4) * 4, me.zl % 4
    far = (me.zl + 4) % 8
    line = lambda zl: cbuf.at[slot_of(zl), :, half]
    sends.start(line(me.zl), line(me.zl), z_s.at[4], z_r.at[4], me.at(zl=far))
    for k in (1, 2, 3):
        sends.start(line(me.zl), line(me.zl), z_s.at[k], z_r.at[k], me.at(zl=base + (pos + k) % 4))
    sends.start(line(me.zl), line(me.zl), b_s.at[0], b_r.at[0], sibling)

    def from_z(k):
        zl = far if k == 4 else base + (pos - k) % 4 if k < 4 else (4 - base) + (pos - (k - 4)) % 4
        return zl

    def along_z(k):
        piece = line(from_z(k))
        arrived(piece, z_r.at[k], sibling)
        if k == 4:
            for i in (1, 2, 3):
                sends.start(piece, piece, z_s.at[4 + i], z_r.at[4 + i], me.at(zl=base + (pos + i) % 4))
        sends.start(piece, piece, b_s.at[k], b_r.at[k], sibling)

    gather_w.level(1)
    for k in (4, 1, 3, 2):
        along_z(k)
    gather_w.level(2)
    arrived(fbuf.at[1 - me.zh, me.y, pl.ds(4 * me.x, 4)], x_r.at[0], sibling)
    own_f.wait()
    fslot = lambda h, px, py: fbuf.at[(me.zh + h) % 2, py, pl.ds(4 * px, 4)]
    gather_f = Gather(me, sends, lambda h: fslot(h, me.x, me.y), fslot, f_s, f_r)
    gather_f.begin(0)
    gather_f.begin(1)
    for k in (5, 7, 6):
        along_z(k)
    for k in range(8):
        zl = me.zl if k == 0 else from_z(k)
        arrived(cbuf.at[slot_of(zl), :, other_half], b_r.at[k], sibling)
    own_w.wait()

    def project(sources):
        total = None
        for i, j in sources:
            px, py = gather_w.source(0, i, j)
            k = py * 4 + px
            a = cbuf[:, :, pl.ds(pl.multiple_of(k * 256, 256), 256)].reshape(128, 256)
            new = jnp.dot(a, wbuf[k], preferred_element_type=jnp.float32)
            total = new if total is None else total + new
        return total.reshape(8, 16, 512)

    gather_w.finish((0, 1), LAST[:4])
    part[...] = project(EARLY)
    gather_w.finish((0, 1), LAST[4:])
    part[...] += project(LATE)
    for k in range(4):
        arrived(rbuf.at[(me.y - k) % 4], e_r.at[k], sibling)
    mine = pl.ds(4 * me.zh, 4)
    part[mine] = part[mine] + rbuf[...].astype(jnp.float32)
    mine_out[...] = part[...].astype(jnp.bfloat16)
    for k in range(4):
        rows = pl.ds(2 * k, 2)
        sends.start(mine_out.at[rows], other.at[rows], x_s.at[1 + k], x_r.at[1 + k], partner)

    sslot = lambda k, px, py: sbuf.at[pl.ds(2 * k, 2), px * 4 + py]
    gather_s = Gather(me, sends, lambda k: sslot(k, me.x, me.y), sslot, s_s, s_r)

    def share(k):
        rows = pl.ds(2 * k, 2)
        arrived(other.at[rows], x_r.at[1 + k], sibling)
        sbuf[rows, me.n] = (part[rows] + other[rows].astype(jnp.float32)).astype(jnp.bfloat16)
        for j in (0, 1):
            px = 2 * me.c + j
            self_here = feeds & (me.y == me.zl // 2) & (me.x == px)
            src, dst = sbuf.at[rows, me.n, :, pl.ds(256 * j, 256)], lbuf.at[rows, me.n]
            sem = t_r.at[k * 16 + me.n]
            sends.start(
                src, dst, t_s.at[k * 2 + j], sem, me.at(y=me.zl // 2, x=px), cond=feeds & jnp.logical_not(self_here)
            )
            pl.when(self_here)(pltpu.make_async_copy(src, dst, sem).start)
        gather_s.begin(k)

    fed = on_line & (me.zl != root)
    above, below = me.zl > root, me.zl < root
    up_hop, down_hop = (8 - root) // 2, (root + 1) // 2
    o_up, o_down = me.zl - root, root - me.zl
    has_up = on_line & (
        ((me.zl == root) & (root < 7))
        | (above & (o_up >= up_hop) & (me.zl < 7))
        | (below & (o_down <= down_hop) & (o_down > 1))
    )
    has_down = on_line & (
        ((me.zl == root) & (root > 0))
        | (below & (o_down >= down_hop) & (me.zl > 0))
        | (above & (o_up <= up_hop) & (o_up > 1))
    )
    at_root = jnp.where(me.zl == root, 1, 0)
    up_zl = jnp.minimum(me.zl + at_root * up_hop + (1 - at_root), 7)
    down_zl = jnp.maximum(me.zl - at_root * down_hop - (1 - at_root), 0)

    depth = jnp.where(above, 1 + jnp.abs(o_up - up_hop), jnp.where(below, 1 + jnp.abs(o_down - down_hop), 0))

    def message(m):
        return lbuf.at[pl.ds(2 * (m // 4), 2), pl.ds(4 * (m % 4), 4)]

    def forwards(m):
        def copy(send, recv, device):
            return pltpu.make_async_remote_copy(
                src_ref=message(m), dst_ref=message(m), send_sem=l_s.at[send], recv_sem=l_r.at[recv],
                device_id=device, device_id_type=MESH,
            )

        up, down = copy(m, m, me.at(zl=up_zl)), copy(16 + m, m, me.at(zl=down_zl))
        return (up, has_up), (down, has_down), (copy(32 + m, 16 + m, sibling), on_line)

    def pass_on(m):
        for copy, cond in forwards(m):
            pl.when(cond)(copy.start)

    def root_sends(k):
        @pl.when(is_root)
        def _():
            for u in range(4):
                for n in range(4 * u, 4 * u + 4):
                    arrived(lbuf.at[pl.ds(2 * k, 2), n], t_r.at[k * 16 + n], sibling)
                pass_on(4 * k + u)

    def take(k, d):
        @pl.when(on_line & (depth == d))
        def _():
            for m in range(4 * k, 4 * k + 4):
                arrived(message(m), l_r.at[m], sibling)
                pass_on(m)

    def from_sibling(k):
        @pl.when(jnp.logical_not(on_line))
        def _():
            for m in range(4 * k, 4 * k + 4):
                arrived(message(m), l_r.at[16 + m], sibling)

    def add(first, parts):
        rows = pl.ds(2 * first, 2 * parts)
        depth_of = parts * 512
        a = lbuf[rows].reshape(depth_of, 256)
        f = fbuf[first // 2, pl.ds(2 * (first % 2), 2 * parts)]
        dims = (((0,), (0,)), ((), ()))
        for out, buf in ((gram, sbuf[rows]), (cross, f)):
            new = lax.dot_general(a, buf.reshape(depth_of, 512), dims, preferred_element_type=jnp.float32) * (1.0 / 2048)
            out[...] = new if first == 0 else out[...] + new

    for slot in range(9):
        if slot == 0:
            gather_f.level(0)
            gather_f.level(1)
        if slot == 1:
            gather_f.level(2)
        if slot < 4:
            share(slot)
        for n in range(3):
            k = slot - 1 - n
            if 0 <= k < 4:
                gather_s.level(n, (k,))
        if 0 <= slot - 1 < 4:
            root_sends(slot - 1)
        for d in range(1, 5):
            k = slot - 1 - d
            if 0 <= k < 4:
                if (k, d) == (3, 4):
                    gather_f.finish()
                    gather_s.finish((0, 1))
                    from_sibling(0)
                    from_sibling(1)
                    add(0, 2)
                    gather_s.finish((2,))
                    from_sibling(2)
                    add(2, 1)
                take(k, d)
    gather_s.finish((3,))
    from_sibling(3)
    add(3, 1)
    for m in range(16):
        for copy, cond in forwards(m):
            pl.when(cond)(copy.wait_send)
    sends.drain()


def body(context, out_weight, residual, final_states):
    vmem, hbm = pl.BlockSpec(memory_space=pltpu.VMEM), pl.BlockSpec(memory_space=pl.ANY)
    dma = lambda n: pltpu.SemaphoreType.DMA((n,))
    bf16, f32 = jnp.bfloat16, jnp.float32
    out = jax.ShapeDtypeStruct((256, 512), f32)
    return pl.pallas_call(
        kernel,
        out_shape=(out, out),
        in_specs=[hbm] * 4,
        out_specs=(vmem, vmem),
        scratch_shapes=[
            pltpu.VMEM((16, 256, 512), bf16),
            pltpu.VMEM((8, 16, 4096), bf16),
            pltpu.VMEM((4, 16, 512), bf16),
            pltpu.VMEM((8, 16, 512), f32),
            pltpu.VMEM((8, 16, 512), bf16),
            pltpu.VMEM((8, 16, 512), bf16),
            pltpu.VMEM((2, 4, 16, 16, 512), bf16),
            pltpu.VMEM((8, 16, 16, 512), bf16),
            pltpu.VMEM((8, 16, 16, 256), bf16),
            dma(32), dma(32), dma(32), dma(32), dma(64), dma(64),
            dma(8), dma(8), dma(8), dma(8), dma(8), dma(8),
            dma(4), dma(4), dma(5), dma(5), dma(8), dma(64), dma(48), dma(32), dma(2),
        ],
        compiler_params=pltpu.CompilerParams(collective_id=0, has_side_effects=True, vmem_limit_bytes=56 << 20),
        cost_estimate=pl.CostEstimate(flops=1 << 31, bytes_accessed=1 << 21, transcendentals=0),
    )(context, out_weight, residual.reshape(4, 16, 512), final_states.reshape(4, 16, 512))


def solution(mesh):
    in_specs = (P("tensor", "dp"), P("dp", "tensor"), P("dp", "tensor"), P("dp", "tensor"))
    out_specs = (P("dp", "tensor"), P("dp", "tensor"))
    return jax.shard_map(body, mesh=mesh, in_specs=in_specs, out_specs=out_specs, check_vma=False)
```

```python
import jax
import jax.numpy as jnp
from jax import lax
from jax.experimental import pallas as pl
from jax.experimental.pallas import tpu as pltpu
from jax.sharding import PartitionSpec as P

MESH = pl.DeviceIdType.MESH
OFFSETS = (0, -1, 1, -2)
LEVELS = (((1, 0), (2, 0), (0, 1)), ((3, 0), (1, 1), (2, 1)), ((3, 1),))
LAST = ((0, 2), (1, 2), (2, 2), (0, 3), (3, 2), (1, 3), (2, 3), (3, 3))
EARLY = ((0, 0), (1, 0), (0, 1), (2, 0), (0, 2), (1, 1), (1, 2), (2, 1), (2, 2), (3, 0), (0, 3))
LATE = ((3, 1), (1, 3), (3, 2), (2, 3), (3, 3))


class Place:
    def __init__(self):
        d, t = lax.axis_index("dp"), lax.axis_index("tensor")
        self.y, self.zh, self.x = d // 8, (d // 4) % 2, d % 4
        self.zl, self.c = t // 2, t % 2
        self.q = self.y * 4 + self.x
        self.n = self.x * 4 + self.y
        self.sg = 1 - 2 * self.c

    def at(self, y=None, zh=None, x=None, zl=None, c=None):
        y, zh, x, zl, c = (b if a is None else a for a, b in zip((y, zh, x, zl, c), (self.y, self.zh, self.x, self.zl, self.c)))
        return y * 8 + zh * 4 + x, zl * 2 + c


class Sends:
    def __init__(self):
        self.pending = []

    def start(self, src, dst, send_sem, recv_sem, device, cond=None):
        copy = pltpu.make_async_remote_copy(
            src_ref=src, dst_ref=dst, send_sem=send_sem, recv_sem=recv_sem, device_id=device, device_id_type=MESH
        )
        if cond is None:
            copy.start()
        else:
            pl.when(cond)(copy.start)
        self.pending.append((copy, cond))

    def drain(self):
        for copy, cond in self.pending:
            if cond is None:
                copy.wait_send()
            else:
                pl.when(cond)(copy.wait_send)
        self.pending = []


def arrived(ref, sem, device):
    pltpu.make_async_remote_copy(
        src_ref=ref, dst_ref=ref, send_sem=sem, recv_sem=sem, device_id=device, device_id_type=MESH
    ).wait_recv()


class Gather:
    def __init__(self, me, sends, own, slot, ssem, rsem):
        self.me, self.sends, self.own, self.slot, self.ssem, self.rsem = me, sends, own, slot, ssem, rsem

    def source(self, h, i, j):
        a, b = (i, j) if h % 2 == 0 else (j, i)
        return (self.me.x + self.me.sg * OFFSETS[a] + 8) % 4, (self.me.y + self.me.sg * OFFSETS[b] + 8) % 4

    def send(self, h, have, give, axis, sign):
        me = self.me
        px, py = self.source(h, *have)
        dst = self.slot(h, px, py)
        src = self.own(h) if have == (0, 0) else dst
        along_x = (axis == 0) == (h % 2 == 0)
        if along_x:
            device = me.at(x=(me.x + sign * me.sg + 4) % 4)
        else:
            device = me.at(y=(me.y + sign * me.sg + 4) % 4)
        k = h * 16 + give[0] * 4 + give[1]
        self.sends.start(src, dst, self.ssem.at[k], self.rsem.at[k], device)

    def begin(self, h):
        self.send(h, (0, 0), (1, 0), 0, 1)
        self.send(h, (0, 0), (2, 0), 0, -1)
        self.send(h, (0, 0), (0, 1), 1, 1)
        self.send(h, (0, 0), (0, 2), 1, -1)

    def event(self, h, i, j):
        px, py = self.source(h, i, j)
        arrived(self.slot(h, px, py), self.rsem.at[h * 16 + i * 4 + j], self.me.at(c=1 - self.me.c))
        if j == 0:
            if i == 1:
                self.send(h, (1, 0), (3, 0), 0, 1)
            self.send(h, (i, 0), (i, 1), 1, 1)
            self.send(h, (i, 0), (i, 2), 1, -1)
        elif j == 1:
            self.send(h, (i, 1), (i, 3), 1, 1)

    def level(self, n, parts=(0, 1)):
        for i, j in LEVELS[n]:
            for h in parts:
                self.event(h, i, j)

    def finish(self, parts=(0, 1), which=LAST):
        for i, j in which:
            for h in parts:
                self.event(h, i, j)


def kernel(
    ctx, w, res, fin, gram, cross,
    wbuf, cbuf, rbuf, part, mine_out, other, fbuf, sbuf, zbuf, lbuf,
    w_s, w_r, f_s, f_r, s_s, s_r, a_s, a_r, z_s, z_r, b_s, b_r, e_s, e_r, x_s, x_r, t_s, t_r, u_s, u_r, l_s, l_r, own_sem,
):
    me = Place()
    sends = Sends()
    sibling = me.at(c=1 - me.c)
    partner = me.at(zh=1 - me.zh)
    lead = me.x // 2
    on_line = me.c == lead
    feeds = me.zl % 2 == me.zh
    other_core = 1 - me.c
    to_core, from_core = me.q // 8, me.x // 2
    swaps_self = (me.x // 2 == me.c) & (me.q // 8 == me.c)

    own_w = pltpu.make_async_copy(w, wbuf.at[me.q], own_sem.at[0])
    own_w.start()
    own_f = pltpu.make_async_copy(fin, fbuf.at[me.zh, me.y, pl.ds(4 * me.x, 4)], own_sem.at[1])
    own_f.start()

    barrier = pltpu.get_barrier_semaphore()

    def greet(device, cond=None):
        signal = lambda: pl.semaphore_signal(barrier, inc=1, device_id=device, device_id_type=MESH)
        if cond is None:
            signal()
        else:
            pl.when(cond)(signal)

    for k in (1, 2, 3):
        greet(me.at(y=(me.y + k) % 4))
    for k in (1, 3):
        greet(me.at(x=(me.x + k) % 4))
    for k in (1, 2, 3):
        greet(me.at(zl=(me.zl // 4) * 4 + (me.zl + k) % 4))
    greet(me.at(zl=(me.zl + 4) % 8))
    greet(partner)
    greet(sibling)
    for i in range(8):
        p = 8 * me.c + i
        greet(me.at(y=p // 4, x=p % 4, c=from_core), jnp.logical_not((p == me.q) & (from_core == me.c)))

    @pl.when(on_line)
    def _():
        for k in range(1, 16):
            p = (me.q + k) % 16
            greet(me.at(y=p // 4, x=p % 4))

    count = 3 + 2 + 4 + 1 + 1 + 8 - jnp.where(swaps_self, 1, 0) + 8 - jnp.where(on_line, 1, 0)
    pl.semaphore_wait(barrier, count)

    slot_of = lambda zl: (zl % 2) * 4 + zl // 2
    lanes = pl.ds(pl.multiple_of(me.q * 256, 256), 256)
    for i in range(8):
        px, py = 2 * me.c + i // 4, i % 4
        src, dst = ctx.at[pl.ds(16 * i, 16)], cbuf.at[slot_of(me.zl), :, lanes]
        k = me.q % 8
        mine = (px == me.x) & (py == me.y) & (to_core == me.c)
        sends.start(src, dst, a_s.at[i], a_r.at[k], me.at(y=py, x=px, c=to_core), cond=jnp.logical_not(mine))
        pl.when(mine)(pltpu.make_async_copy(src, dst, a_r.at[k]).start)

    gather_w = Gather(
        me, sends,
        lambda h: w.at[pl.ds(128 * h, 128)],
        lambda h, px, py: wbuf.at[py * 4 + px, pl.ds(128 * h, 128)],
        w_s, w_r,
    )
    gather_w.begin(0)
    gather_w.begin(1)
    sends.start(fin, fbuf.at[me.zh, me.y, pl.ds(4 * me.x, 4)], x_s.at[0], x_r.at[0], partner)

    for k in range(4):
        j = (me.y + k) % 4
        if k == 0:
            pltpu.make_async_copy(res.at[j], rbuf.at[me.y], e_r.at[0]).start()
        else:
            sends.start(res.at[j], rbuf.at[me.y], e_s.at[k], e_r.at[k], me.at(y=j))

    half = pl.ds(pl.multiple_of(me.c * 2048, 2048), 2048)
    other_half = pl.ds(pl.multiple_of(other_core * 2048, 2048), 2048)
    gather_w.level(0)
    for i in range(8):
        piece = cbuf.at[slot_of(me.zl), :, pl.ds(pl.multiple_of((me.c * 8 + i) * 256, 256), 256)]
        arrived(piece, a_r.at[i], sibling)

    base, pos = (me.zl // 4) * 4, me.zl % 4
    far = (me.zl + 4) % 8
    line = lambda zl: cbuf.at[slot_of(zl), :, half]
    sends.start(line(me.zl), line(me.zl), z_s.at[4], z_r.at[4], me.at(zl=far))
    for k in (1, 2, 3):
        sends.start(line(me.zl), line(me.zl), z_s.at[k], z_r.at[k], me.at(zl=base + (pos + k) % 4))
    sends.start(line(me.zl), line(me.zl), b_s.at[0], b_r.at[0], sibling)

    def from_z(k):
        zl = far if k == 4 else base + (pos - k) % 4 if k < 4 else (4 - base) + (pos - (k - 4)) % 4
        return zl

    def along_z(k):
        piece = line(from_z(k))
        arrived(piece, z_r.at[k], sibling)
        if k == 4:
            for i in (1, 2, 3):
                sends.start(piece, piece, z_s.at[4 + i], z_r.at[4 + i], me.at(zl=base + (pos + i) % 4))
        sends.start(piece, piece, b_s.at[k], b_r.at[k], sibling)

    gather_w.level(1)
    for k in (4, 1, 3, 2):
        along_z(k)
    gather_w.level(2)
    arrived(fbuf.at[1 - me.zh, me.y, pl.ds(4 * me.x, 4)], x_r.at[0], sibling)
    own_f.wait()
    fslot = lambda h, px, py: fbuf.at[(me.zh + h) % 2, py, pl.ds(4 * px, 4)]
    gather_f = Gather(me, sends, lambda h: fslot(h, me.x, me.y), fslot, f_s, f_r)
    gather_f.begin(0)
    gather_f.begin(1)
    for k in (5, 7, 6):
        along_z(k)
    for k in range(8):
        zl = me.zl if k == 0 else from_z(k)
        arrived(cbuf.at[slot_of(zl), :, other_half], b_r.at[k], sibling)
    own_w.wait()

    def project(sources):
        total = None
        for i, j in sources:
            px, py = gather_w.source(0, i, j)
            k = py * 4 + px
            a = cbuf[:, :, pl.ds(pl.multiple_of(k * 256, 256), 256)].reshape(128, 256)
            new = jnp.dot(a, wbuf[k], preferred_element_type=jnp.float32)
            total = new if total is None else total + new
        return total.reshape(8, 16, 512)

    gather_w.finish((0, 1), LAST[:4])
    part[...] = project(EARLY)
    gather_w.finish((0, 1), LAST[4:])
    part[...] += project(LATE)
    for k in range(4):
        arrived(rbuf.at[(me.y - k) % 4], e_r.at[k], sibling)
    mine = pl.ds(4 * me.zh, 4)
    part[mine] = part[mine] + rbuf[...].astype(jnp.float32)
    mine_out[...] = part[...].astype(jnp.bfloat16)
    for k in range(4):
        rows = pl.ds(2 * k, 2)
        sends.start(mine_out.at[rows], other.at[rows], x_s.at[1 + k], x_r.at[1 + k], partner)

    sslot = lambda k, px, py: sbuf.at[pl.ds(2 * k, 2), px * 4 + py]
    gather_s = Gather(me, sends, lambda k: sslot(k, me.x, me.y), sslot, s_s, s_r)

    def share(k):
        rows = pl.ds(2 * k, 2)
        arrived(other.at[rows], x_r.at[1 + k], sibling)
        new = (part[rows] + other[rows].astype(jnp.float32)).astype(jnp.bfloat16)
        sbuf[rows, me.n] = new

        @pl.when(feeds)
        def _():
            zbuf[me.zl // 2, rows] = new

        piece = zbuf.at[me.zl // 2, rows]
        recv = u_r.at[k * 4 + me.zl // 2]
        sends.start(piece, piece, u_s.at[k * 7], recv, me.at(zl=far), cond=feeds)
        for i in (1, 2, 3):
            sends.start(piece, piece, u_s.at[k * 7 + i], recv, me.at(zl=base + (pos + i) % 4), cond=feeds)
        gather_s.begin(k)

    def pass_along_z(k):
        piece = zbuf.at[far // 2, pl.ds(2 * k, 2)]
        recv = u_r.at[k * 4 + far // 2]
        pl.when(feeds)(lambda: arrived(piece, recv, sibling))
        for i in (1, 2, 3):
            sends.start(piece, piece, u_s.at[k * 7 + 3 + i], recv, me.at(zl=base + (pos + i) % 4), cond=feeds)

    def swap(k):
        rows = pl.ds(2 * k, 2)
        for p in range(4):
            had = feeds & ((me.zl // 2 == p) | (far // 2 == p))
            pl.when(jnp.logical_not(had))(lambda: arrived(zbuf.at[p, rows], u_r.at[k * 4 + p], sibling))
            for j in (0, 1):
                px = 2 * me.c + j
                here = (me.y == p) & (me.x == px)
                src, dst = zbuf.at[p, rows, :, pl.ds(256 * j, 256)], lbuf.at[rows, me.n]
                sends.start(
                    src, dst, t_s.at[k * 8 + p * 2 + j], t_r.at[k], me.at(y=p, x=px), cond=jnp.logical_not(here)
                )
                pl.when(here)(pltpu.make_async_copy(src, dst, t_r.at[k]).start)

    def to_sibling(k):
        piece = lbuf.at[pl.ds(2 * k, 2)]
        pl.when(on_line)(lambda: arrived(piece, t_r.at[k], sibling))
        sends.start(piece, piece, l_s.at[k], l_r.at[k], sibling, cond=on_line)

    def from_sibling(k):
        pl.when(jnp.logical_not(on_line))(lambda: arrived(lbuf.at[pl.ds(2 * k, 2)], l_r.at[k], sibling))

    def add(first, parts):
        rows = pl.ds(2 * first, 2 * parts)
        depth_of = parts * 512
        a = lbuf[rows].reshape(depth_of, 256)
        f = fbuf[first // 2, pl.ds(2 * (first % 2), 2 * parts)]
        dims = (((0,), (0,)), ((), ()))
        for out, buf in ((gram, sbuf[rows]), (cross, f)):
            new = lax.dot_general(a, buf.reshape(depth_of, 512), dims, preferred_element_type=jnp.float32) * (1.0 / 2048)
            out[...] = new if first == 0 else out[...] + new

    for slot in range(9):
        if slot == 0:
            gather_f.level(0)
            gather_f.level(1)
        if slot == 1:
            gather_f.level(2)
        if slot < 4:
            share(slot)
        for n in range(3):
            k = slot - 1 - n
            if 0 <= k < 4:
                gather_s.level(n, (k,))
        if 0 <= slot - 1 < 4:
            pass_along_z(slot - 1)
        if 0 <= slot - 2 < 4:
            swap(slot - 2)
        if 0 <= slot - 5 < 4:
            to_sibling(slot - 5)
        if slot == 7:
            gather_f.finish()
            gather_s.finish((0, 1))
            from_sibling(0)
            from_sibling(1)
            add(0, 2)
    gather_s.finish((2,))
    from_sibling(2)
    add(2, 1)
    gather_s.finish((3,))
    from_sibling(3)
    add(3, 1)
    sends.drain()


def body(context, out_weight, residual, final_states):
    vmem, hbm = pl.BlockSpec(memory_space=pltpu.VMEM), pl.BlockSpec(memory_space=pl.ANY)
    dma = lambda n: pltpu.SemaphoreType.DMA((n,))
    bf16, f32 = jnp.bfloat16, jnp.float32
    out = jax.ShapeDtypeStruct((256, 512), f32)
    return pl.pallas_call(
        kernel,
        out_shape=(out, out),
        in_specs=[hbm] * 4,
        out_specs=(vmem, vmem),
        scratch_shapes=[
            pltpu.VMEM((16, 256, 512), bf16),
            pltpu.VMEM((8, 16, 4096), bf16),
            pltpu.VMEM((4, 16, 512), bf16),
            pltpu.VMEM((8, 16, 512), f32),
            pltpu.VMEM((8, 16, 512), bf16),
            pltpu.VMEM((8, 16, 512), bf16),
            pltpu.VMEM((2, 4, 16, 16, 512), bf16),
            pltpu.VMEM((8, 16, 16, 512), bf16),
            pltpu.VMEM((4, 8, 16, 512), bf16),
            pltpu.VMEM((8, 16, 16, 256), bf16),
            dma(32), dma(32), dma(32), dma(32), dma(64), dma(64),
            dma(8), dma(8), dma(8), dma(8), dma(8), dma(8),
            dma(4), dma(4), dma(5), dma(5), dma(32), dma(4), dma(28), dma(16), dma(4), dma(4), dma(2),
        ],
        compiler_params=pltpu.CompilerParams(collective_id=0, has_side_effects=True, vmem_limit_bytes=56 << 20),
        cost_estimate=pl.CostEstimate(flops=1 << 31, bytes_accessed=1 << 21, transcendentals=0),
    )(context, out_weight, residual.reshape(4, 16, 512), final_states.reshape(4, 16, 512))


def solution(mesh):
    in_specs = (P("tensor", "dp"), P("dp", "tensor"), P("dp", "tensor"), P("dp", "tensor"))
    out_specs = (P("dp", "tensor"), P("dp", "tensor"))
    return jax.shard_map(body, mesh=mesh, in_specs=in_specs, out_specs=out_specs, check_vma=False)
```

```python
import jax
import jax.numpy as jnp
from jax import lax
from jax.experimental import pallas as pl
from jax.experimental.pallas import tpu as pltpu
from jax.sharding import PartitionSpec as P

MESH = pl.DeviceIdType.MESH
OFFSETS = (0, -1, 1, -2)
LEVELS = (((1, 0), (2, 0), (0, 1)), ((3, 0), (1, 1), (2, 1)), ((3, 1),))
LAST = ((0, 2), (1, 2), (2, 2), (0, 3), (3, 2), (1, 3), (2, 3), (3, 3))
EARLY = ((0, 0), (1, 0), (0, 1), (2, 0), (0, 2), (1, 1), (1, 2), (2, 1), (2, 2), (3, 0), (0, 3))
LATE = ((3, 1), (1, 3), (3, 2), (2, 3), (3, 3))


TREES = {
    0: {0: (5, 2, 1), 5: (7, 6, 4), 2: (3,)},
    2: {2: (7, 3, 1), 7: (6, 5), 3: (4,), 1: (0,)},
    4: {4: (1, 3, 6, 5), 1: (0,), 3: (2,), 6: (7,)},
    6: {6: (1, 4, 5, 7), 1: (0, 2), 4: (3,)},
}


class Place:
    def __init__(self):
        d, t = lax.axis_index("dp"), lax.axis_index("tensor")
        self.y, self.zh, self.x = d // 8, (d // 4) % 2, d % 4
        self.zl, self.c = t // 2, t % 2
        self.q = self.y * 4 + self.x
        self.n = self.x * 4 + self.y
        self.sg = 1 - 2 * self.c

    def at(self, y=None, zh=None, x=None, zl=None, c=None):
        y, zh, x, zl, c = (b if a is None else a for a, b in zip((y, zh, x, zl, c), (self.y, self.zh, self.x, self.zl, self.c)))
        return y * 8 + zh * 4 + x, zl * 2 + c


class Sends:
    def __init__(self):
        self.pending = []

    def start(self, src, dst, send_sem, recv_sem, device, cond=None):
        copy = pltpu.make_async_remote_copy(
            src_ref=src, dst_ref=dst, send_sem=send_sem, recv_sem=recv_sem, device_id=device, device_id_type=MESH
        )
        if cond is None:
            copy.start()
        else:
            pl.when(cond)(copy.start)
        self.pending.append((copy, cond))

    def drain(self):
        for copy, cond in self.pending:
            if cond is None:
                copy.wait_send()
            else:
                pl.when(cond)(copy.wait_send)
        self.pending = []


def arrived(ref, sem, device):
    pltpu.make_async_remote_copy(
        src_ref=ref, dst_ref=ref, send_sem=sem, recv_sem=sem, device_id=device, device_id_type=MESH
    ).wait_recv()


class Gather:
    def __init__(self, me, sends, own, slot, ssem, rsem):
        self.me, self.sends, self.own, self.slot, self.ssem, self.rsem = me, sends, own, slot, ssem, rsem

    def source(self, h, i, j):
        a, b = (i, j) if h % 2 == 0 else (j, i)
        return (self.me.x + self.me.sg * OFFSETS[a] + 8) % 4, (self.me.y + self.me.sg * OFFSETS[b] + 8) % 4

    def send(self, h, have, give, axis, sign):
        me = self.me
        px, py = self.source(h, *have)
        dst = self.slot(h, px, py)
        src = self.own(h) if have == (0, 0) else dst
        along_x = (axis == 0) == (h % 2 == 0)
        if along_x:
            device = me.at(x=(me.x + sign * me.sg + 4) % 4)
        else:
            device = me.at(y=(me.y + sign * me.sg + 4) % 4)
        k = h * 16 + give[0] * 4 + give[1]
        self.sends.start(src, dst, self.ssem.at[k], self.rsem.at[k], device)

    def begin(self, h):
        self.send(h, (0, 0), (1, 0), 0, 1)
        self.send(h, (0, 0), (2, 0), 0, -1)
        self.send(h, (0, 0), (0, 1), 1, 1)
        self.send(h, (0, 0), (0, 2), 1, -1)

    def event(self, h, i, j):
        px, py = self.source(h, i, j)
        arrived(self.slot(h, px, py), self.rsem.at[h * 16 + i * 4 + j], self.me.at(c=1 - self.me.c))
        if j == 0:
            if i == 1:
                self.send(h, (1, 0), (3, 0), 0, 1)
            self.send(h, (i, 0), (i, 1), 1, 1)
            self.send(h, (i, 0), (i, 2), 1, -1)
        elif j == 1:
            self.send(h, (i, 1), (i, 3), 1, 1)

    def level(self, n, parts=(0, 1)):
        for i, j in LEVELS[n]:
            for h in parts:
                self.event(h, i, j)

    def finish(self, parts=(0, 1), which=LAST):
        for i, j in which:
            for h in parts:
                self.event(h, i, j)


def kernel(
    ctx, w, res, fin, gram, cross,
    wbuf, cbuf, rbuf, part, mine_out, other, fbuf, sbuf, zbuf, lbuf,
    w_s, w_r, f_s, f_r, s_s, s_r, a_s, a_r, z_s, z_r, b_s, b_r, e_s, e_r, x_s, x_r, t_s, t_r, u_s, u_r, l_s, l_r, own_sem,
):
    me = Place()
    sends = Sends()
    sibling = me.at(c=1 - me.c)
    partner = me.at(zh=1 - me.zh)
    lead = me.x // 2
    on_line = me.c == lead
    feeds = me.zl % 2 == me.zh
    other_core = 1 - me.c
    to_core, from_core = me.q // 8, me.x // 2

    own_w = pltpu.make_async_copy(w, wbuf.at[me.q], own_sem.at[0])
    own_w.start()
    own_f = pltpu.make_async_copy(fin, fbuf.at[me.zh, me.y, pl.ds(4 * me.x, 4)], own_sem.at[1])
    own_f.start()

    barrier = pltpu.get_barrier_semaphore()

    def greet(device, cond=None):
        signal = lambda: pl.semaphore_signal(barrier, inc=1, device_id=device, device_id_type=MESH)
        if cond is None:
            signal()
        else:
            pl.when(cond)(signal)

    for k in range(1, 8):
        greet(me.at(zl=(me.zl + k) % 8))
    greet(partner)
    greet(sibling)

    @pl.when(on_line)
    def _():
        for k in range(1, 16):
            p = (me.q + k) % 16
            greet(me.at(y=p // 4, x=p % 4))

    @pl.when(jnp.logical_not(on_line))
    def _():
        for k in (1, 2, 3):
            greet(me.at(y=(me.y + k) % 4))
        for k in (1, 3):
            greet(me.at(x=(me.x + k) % 4))
        for i in range(8):
            p = 8 * me.c + i
            greet(me.at(y=p // 4, x=p % 4, c=from_core))

    count = 7 + 1 + 1 + 8 + 1 + jnp.where(on_line, -1, 3) + jnp.where(to_core == me.c, 0, 8)
    pl.semaphore_wait(barrier, count)

    slot_of = lambda zl: (zl % 2) * 4 + zl // 2
    lanes = pl.ds(pl.multiple_of(me.q * 256, 256), 256)
    for i in range(8):
        px, py = 2 * me.c + i // 4, i % 4
        src, dst = ctx.at[pl.ds(16 * i, 16)], cbuf.at[slot_of(me.zl), :, lanes]
        k = me.q % 8
        mine = (px == me.x) & (py == me.y) & (to_core == me.c)
        sends.start(src, dst, a_s.at[i], a_r.at[k], me.at(y=py, x=px, c=to_core), cond=jnp.logical_not(mine))
        pl.when(mine)(pltpu.make_async_copy(src, dst, a_r.at[k]).start)

    gather_w = Gather(
        me, sends,
        lambda h: w.at[pl.ds(128 * h, 128)],
        lambda h, px, py: wbuf.at[py * 4 + px, pl.ds(128 * h, 128)],
        w_s, w_r,
    )
    gather_w.begin(0)
    gather_w.begin(1)
    sends.start(fin, fbuf.at[me.zh, me.y, pl.ds(4 * me.x, 4)], x_s.at[0], x_r.at[0], partner)

    for k in range(4):
        j = (me.y + k) % 4
        if k == 0:
            pltpu.make_async_copy(res.at[j], rbuf.at[me.y], e_r.at[0]).start()
        else:
            sends.start(res.at[j], rbuf.at[me.y], e_s.at[k], e_r.at[k], me.at(y=j))

    half = pl.ds(pl.multiple_of(me.c * 2048, 2048), 2048)
    other_half = pl.ds(pl.multiple_of(other_core * 2048, 2048), 2048)
    gather_w.level(0)
    for i in range(8):
        piece = cbuf.at[slot_of(me.zl), :, pl.ds(pl.multiple_of((me.c * 8 + i) * 256, 256), 256)]
        arrived(piece, a_r.at[i], sibling)

    base, pos = (me.zl // 4) * 4, me.zl % 4
    far = (me.zl + 4) % 8
    line = lambda zl: cbuf.at[slot_of(zl), :, half]
    sends.start(line(me.zl), line(me.zl), z_s.at[4], z_r.at[4], me.at(zl=far))
    for k in (1, 2, 3):
        sends.start(line(me.zl), line(me.zl), z_s.at[k], z_r.at[k], me.at(zl=base + (pos + k) % 4))
    sends.start(line(me.zl), line(me.zl), b_s.at[0], b_r.at[0], sibling)

    def from_z(k):
        zl = far if k == 4 else base + (pos - k) % 4 if k < 4 else (4 - base) + (pos - (k - 4)) % 4
        return zl

    def along_z(k):
        piece = line(from_z(k))
        arrived(piece, z_r.at[k], sibling)
        if k == 4:
            for i in (1, 2, 3):
                sends.start(piece, piece, z_s.at[4 + i], z_r.at[4 + i], me.at(zl=base + (pos + i) % 4))
        sends.start(piece, piece, b_s.at[k], b_r.at[k], sibling)

    gather_w.level(1)
    for k in (4, 1, 3, 2):
        along_z(k)
    gather_w.level(2)
    arrived(fbuf.at[1 - me.zh, me.y, pl.ds(4 * me.x, 4)], x_r.at[0], sibling)
    own_f.wait()
    fslot = lambda h, px, py: fbuf.at[(me.zh + h) % 2, py, pl.ds(4 * px, 4)]
    gather_f = Gather(me, sends, lambda h: fslot(h, me.x, me.y), fslot, f_s, f_r)
    gather_f.begin(0)
    gather_f.begin(1)
    for k in (5, 7, 6):
        along_z(k)
    for k in range(8):
        zl = me.zl if k == 0 else from_z(k)
        arrived(cbuf.at[slot_of(zl), :, other_half], b_r.at[k], sibling)
    own_w.wait()

    def project(sources):
        total = None
        for i, j in sources:
            px, py = gather_w.source(0, i, j)
            k = py * 4 + px
            a = cbuf[:, :, pl.ds(pl.multiple_of(k * 256, 256), 256)].reshape(128, 256)
            new = jnp.dot(a, wbuf[k], preferred_element_type=jnp.float32)
            total = new if total is None else total + new
        return total.reshape(8, 16, 512)

    gather_w.finish((0, 1), LAST[:4])
    part[...] = project(EARLY)
    gather_w.finish((0, 1), LAST[4:])
    part[...] += project(LATE)
    for k in range(4):
        arrived(rbuf.at[(me.y - k) % 4], e_r.at[k], sibling)
    mine = pl.ds(4 * me.zh, 4)
    part[mine] = part[mine] + rbuf[...].astype(jnp.float32)
    mine_out[...] = part[...].astype(jnp.bfloat16)
    for k in range(4):
        rows = pl.ds(2 * k, 2)
        sends.start(mine_out.at[rows], other.at[rows], x_s.at[1 + k], x_r.at[1 + k], partner)

    sslot = lambda k, px, py: sbuf.at[pl.ds(2 * k, 2), px * 4 + py]
    gather_s = Gather(me, sends, lambda k: sslot(k, me.x, me.y), sslot, s_s, s_r)

    def share(k):
        rows = pl.ds(2 * k, 2)
        arrived(other.at[rows], x_r.at[1 + k], sibling)
        new = (part[rows] + other[rows].astype(jnp.float32)).astype(jnp.bfloat16)
        sbuf[rows, me.n] = new

        @pl.when(feeds)
        def _():
            zbuf[me.zl // 2, rows] = new

        for v in (0, 2, 4, 6):

            @pl.when(spot == v)
            def _():
                for copy in line_copies(k, v, v):
                    copy.start()

        gather_s.begin(k)

    mirror = lambda v: v + me.zh * (7 - 2 * v)
    spot = mirror(me.zl)
    row_of = lambda source: source // 2 + me.zh * (3 - 2 * (source // 2))

    def line_copies(k, v, source):
        piece = zbuf.at[row_of(source), pl.ds(2 * k, 2)]
        return [
            pltpu.make_async_remote_copy(
                src_ref=piece, dst_ref=piece, send_sem=u_s.at[k * 16 + source * 2 + i], recv_sem=u_r.at[k * 4 + source // 2],
                device_id=me.at(zl=mirror(child)), device_id_type=MESH,
            )
            for i, child in enumerate(TREES[source].get(v, ()))
        ]

    def pass_along_z(k):
        for v in range(1, 8):

            @pl.when(spot == v)
            def _():
                for source in TREES:
                    if v != source and v in TREES[source]:
                        arrived(zbuf.at[row_of(source), pl.ds(2 * k, 2)], u_r.at[k * 4 + source // 2], sibling)
                        for copy in line_copies(k, v, source):
                            copy.start()

    def sent_along_z():
        for v in range(8):

            @pl.when(spot == v)
            def _():
                for k in range(4):
                    for source in TREES:
                        for copy in line_copies(k, v, source):
                            copy.wait_send()

    def swap(k):
        rows = pl.ds(2 * k, 2)
        for source in TREES:
            p = row_of(source)
            had = False
            for v in TREES[source]:
                had = had | (spot == v)
            pl.when(jnp.logical_not(had))(lambda: arrived(zbuf.at[p, rows], u_r.at[k * 4 + source // 2], sibling))
            for j in (0, 1):
                px = 2 * me.c + j
                here = (me.y == p) & (me.x == px)
                src, dst = zbuf.at[p, rows, :, pl.ds(256 * j, 256)], lbuf.at[rows, me.n]
                sends.start(
                    src, dst, t_s.at[k * 8 + source + j], t_r.at[k], me.at(y=p, x=px), cond=jnp.logical_not(here)
                )
                pl.when(here)(pltpu.make_async_copy(src, dst, t_r.at[k]).start)

    def to_sibling(k):
        piece = lbuf.at[pl.ds(2 * k, 2)]
        pl.when(on_line)(lambda: arrived(piece, t_r.at[k], sibling))
        sends.start(piece, piece, l_s.at[k], l_r.at[k], sibling, cond=on_line)

    def from_sibling(k):
        pl.when(jnp.logical_not(on_line))(lambda: arrived(lbuf.at[pl.ds(2 * k, 2)], l_r.at[k], sibling))

    def add(first, parts):
        rows = pl.ds(2 * first, 2 * parts)
        depth_of = parts * 512
        a = lbuf[rows].reshape(depth_of, 256)
        f = fbuf[first // 2, pl.ds(2 * (first % 2), 2 * parts)]
        dims = (((0,), (0,)), ((), ()))
        for out, buf in ((gram, sbuf[rows]), (cross, f)):
            new = lax.dot_general(a, buf.reshape(depth_of, 512), dims, preferred_element_type=jnp.float32) * (1.0 / 2048)
            out[...] = new if first == 0 else out[...] + new

    for slot in range(9):
        if slot == 0:
            gather_f.level(0)
            gather_f.level(1)
        if slot == 1:
            gather_f.level(2)
        if slot < 4:
            share(slot)
        for n in range(3):
            k = slot - 1 - n
            if 0 <= k < 4:
                gather_s.level(n, (k,))
        if 0 <= slot - 1 < 4:
            pass_along_z(slot - 1)
        if 0 <= slot - 2 < 4:
            swap(slot - 2)
        if 0 <= slot - 5 < 4:
            to_sibling(slot - 5)
        if slot == 7:
            gather_f.finish()
            gather_s.finish((0, 1))
            from_sibling(0)
            from_sibling(1)
            add(0, 2)
    gather_s.finish((2,))
    from_sibling(2)
    add(2, 1)
    gather_s.finish((3,))
    from_sibling(3)
    add(3, 1)
    sent_along_z()
    sends.drain()


def body(context, out_weight, residual, final_states):
    vmem, hbm = pl.BlockSpec(memory_space=pltpu.VMEM), pl.BlockSpec(memory_space=pl.ANY)
    dma = lambda n: pltpu.SemaphoreType.DMA((n,))
    bf16, f32 = jnp.bfloat16, jnp.float32
    out = jax.ShapeDtypeStruct((256, 512), f32)
    return pl.pallas_call(
        kernel,
        out_shape=(out, out),
        in_specs=[hbm] * 4,
        out_specs=(vmem, vmem),
        scratch_shapes=[
            pltpu.VMEM((16, 256, 512), bf16),
            pltpu.VMEM((8, 16, 4096), bf16),
            pltpu.VMEM((4, 16, 512), bf16),
            pltpu.VMEM((8, 16, 512), f32),
            pltpu.VMEM((8, 16, 512), bf16),
            pltpu.VMEM((8, 16, 512), bf16),
            pltpu.VMEM((2, 4, 16, 16, 512), bf16),
            pltpu.VMEM((8, 16, 16, 512), bf16),
            pltpu.VMEM((4, 8, 16, 512), bf16),
            pltpu.VMEM((8, 16, 16, 256), bf16),
            dma(32), dma(32), dma(32), dma(32), dma(64), dma(64),
            dma(8), dma(8), dma(8), dma(8), dma(8), dma(8),
            dma(4), dma(4), dma(5), dma(5), dma(32), dma(4), dma(64), dma(16), dma(4), dma(4), dma(2),
        ],
        compiler_params=pltpu.CompilerParams(collective_id=0, has_side_effects=True, vmem_limit_bytes=56 << 20),
        cost_estimate=pl.CostEstimate(flops=1 << 31, bytes_accessed=1 << 21, transcendentals=0),
    )(context, out_weight, residual.reshape(4, 16, 512), final_states.reshape(4, 16, 512))


def solution(mesh):
    in_specs = (P("tensor", "dp"), P("dp", "tensor"), P("dp", "tensor"), P("dp", "tensor"))
    out_specs = (P("dp", "tensor"), P("dp", "tensor"))
    return jax.shard_map(body, mesh=mesh, in_specs=in_specs, out_specs=out_specs, check_vma=False)
```

```python
import jax
import jax.numpy as jnp
from jax import lax
from jax.experimental import pallas as pl
from jax.experimental.pallas import tpu as pltpu
from jax.sharding import PartitionSpec as P

MESH = pl.DeviceIdType.MESH
OFFSETS = (0, -1, 1, -2)
LEVELS = (((1, 0), (2, 0), (0, 1)), ((3, 0), (1, 1), (2, 1)), ((3, 1),))
LAST = ((0, 2), (1, 2), (2, 2), (0, 3), (3, 2), (1, 3), (2, 3), (3, 3))
EARLY = ((0, 0), (1, 0), (0, 1), (2, 0), (0, 2), (1, 1), (1, 2), (2, 1), (2, 2), (3, 0), (0, 3))
LATE = ((3, 1), (1, 3), (3, 2), (2, 3), (3, 3))


TREES = {
    0: {0: (5, 2, 1), 5: (7, 6, 4), 2: (3,)},
    2: {2: (7, 3, 1), 7: (6, 5), 3: (4,), 1: (0,)},
    4: {4: (1, 3, 6, 5), 1: (0,), 3: (2,), 6: (7,)},
    6: {6: (1, 4, 5, 7), 1: (0, 2), 4: (3,)},
}


class Place:
    def __init__(self):
        d, t = lax.axis_index("dp"), lax.axis_index("tensor")
        self.y, self.zh, self.x = d // 8, (d // 4) % 2, d % 4
        self.zl, self.c = t // 2, t % 2
        self.q = self.y * 4 + self.x
        self.n = self.x * 4 + self.y
        self.sg = 1 - 2 * self.c

    def at(self, y=None, zh=None, x=None, zl=None, c=None):
        y, zh, x, zl, c = (b if a is None else a for a, b in zip((y, zh, x, zl, c), (self.y, self.zh, self.x, self.zl, self.c)))
        return y * 8 + zh * 4 + x, zl * 2 + c


class Sends:
    def __init__(self):
        self.pending = []

    def start(self, src, dst, send_sem, recv_sem, device, cond=None):
        copy = pltpu.make_async_remote_copy(
            src_ref=src, dst_ref=dst, send_sem=send_sem, recv_sem=recv_sem, device_id=device, device_id_type=MESH
        )
        if cond is None:
            copy.start()
        else:
            pl.when(cond)(copy.start)
        self.pending.append((copy, cond))

    def drain(self):
        for copy, cond in self.pending:
            if cond is None:
                copy.wait_send()
            else:
                pl.when(cond)(copy.wait_send)
        self.pending = []


def arrived(ref, sem, device):
    pltpu.make_async_remote_copy(
        src_ref=ref, dst_ref=ref, send_sem=sem, recv_sem=sem, device_id=device, device_id_type=MESH
    ).wait_recv()


class Gather:
    def __init__(self, me, sends, own, slot, ssem, rsem):
        self.me, self.sends, self.own, self.slot, self.ssem, self.rsem = me, sends, own, slot, ssem, rsem

    def source(self, h, i, j):
        a, b = (i, j) if h % 2 == 0 else (j, i)
        return (self.me.x + self.me.sg * OFFSETS[a] + 8) % 4, (self.me.y + self.me.sg * OFFSETS[b] + 8) % 4

    def send(self, h, have, give, axis, sign):
        me = self.me
        px, py = self.source(h, *have)
        dst = self.slot(h, px, py)
        src = self.own(h) if have == (0, 0) else dst
        along_x = (axis == 0) == (h % 2 == 0)
        if along_x:
            device = me.at(x=(me.x + sign * me.sg + 4) % 4)
        else:
            device = me.at(y=(me.y + sign * me.sg + 4) % 4)
        k = h * 16 + give[0] * 4 + give[1]
        self.sends.start(src, dst, self.ssem.at[k], self.rsem.at[k], device)

    def begin(self, h):
        self.send(h, (0, 0), (1, 0), 0, 1)
        self.send(h, (0, 0), (2, 0), 0, -1)
        self.send(h, (0, 0), (0, 1), 1, 1)
        self.send(h, (0, 0), (0, 2), 1, -1)

    def event(self, h, i, j):
        px, py = self.source(h, i, j)
        arrived(self.slot(h, px, py), self.rsem.at[h * 16 + i * 4 + j], self.me.at(c=1 - self.me.c))
        if j == 0:
            if i == 1:
                self.send(h, (1, 0), (3, 0), 0, 1)
            self.send(h, (i, 0), (i, 1), 1, 1)
            self.send(h, (i, 0), (i, 2), 1, -1)
        elif j == 1:
            self.send(h, (i, 1), (i, 3), 1, 1)

    def level(self, n, parts=(0, 1)):
        for i, j in LEVELS[n]:
            for h in parts:
                self.event(h, i, j)

    def finish(self, parts=(0, 1), which=LAST):
        for i, j in which:
            for h in parts:
                self.event(h, i, j)


def kernel(
    ctx, w, res, fin, gram, cross,
    wbuf, cbuf, rbuf, part, mine_out, other, fbuf, sbuf, zbuf, lbuf,
    w_s, w_r, f_s, f_r, s_s, s_r, a_s, a_r, z_s, z_r, b_s, b_r, e_s, e_r, x_s, x_r, t_s, t_r, u_s, u_r, l_s, l_r, own_sem,
):
    me = Place()
    sends = Sends()
    sibling = me.at(c=1 - me.c)
    partner = me.at(zh=1 - me.zh)
    lead = me.x // 2
    on_line = me.c == lead
    feeds = me.zl % 2 == me.zh
    other_core = 1 - me.c
    to_core, from_core = me.q // 8, me.x // 2

    own_w = pltpu.make_async_copy(w, wbuf.at[me.q], own_sem.at[0])
    own_w.start()
    own_f = pltpu.make_async_copy(fin, fbuf.at[me.zh, me.y, pl.ds(4 * me.x, 4)], own_sem.at[1])
    own_f.start()

    barrier = pltpu.get_barrier_semaphore()

    def greet(device, cond=None):
        signal = lambda: pl.semaphore_signal(barrier, inc=1, device_id=device, device_id_type=MESH)
        if cond is None:
            signal()
        else:
            pl.when(cond)(signal)

    for k in range(1, 8):
        greet(me.at(zl=(me.zl + k) % 8))
    greet(partner)
    greet(sibling)

    @pl.when(on_line)
    def _():
        for k in range(1, 16):
            p = (me.q + k) % 16
            greet(me.at(y=p // 4, x=p % 4))

    @pl.when(jnp.logical_not(on_line))
    def _():
        for k in (1, 2, 3):
            greet(me.at(y=(me.y + k) % 4))
        for k in (1, 3):
            greet(me.at(x=(me.x + k) % 4))
        for i in range(8):
            p = 8 * me.c + i
            greet(me.at(y=p // 4, x=p % 4, c=from_core))

    count = 7 + 1 + 1 + 8 + 1 + jnp.where(on_line, -1, 3) + jnp.where(to_core == me.c, 0, 8)
    pl.semaphore_wait(barrier, count)

    slot_of = lambda zl: (zl % 2) * 4 + zl // 2
    lanes = pl.ds(pl.multiple_of(me.q * 256, 256), 256)
    for i in range(8):
        px, py = 2 * me.c + i // 4, i % 4
        src, dst = ctx.at[pl.ds(16 * i, 16)], cbuf.at[slot_of(me.zl), :, lanes]
        k = me.q % 8
        mine = (px == me.x) & (py == me.y) & (to_core == me.c)
        sends.start(src, dst, a_s.at[i], a_r.at[k], me.at(y=py, x=px, c=to_core), cond=jnp.logical_not(mine))
        pl.when(mine)(pltpu.make_async_copy(src, dst, a_r.at[k]).start)

    gather_w = Gather(
        me, sends,
        lambda h: w.at[pl.ds(128 * h, 128)],
        lambda h, px, py: wbuf.at[py * 4 + px, pl.ds(128 * h, 128)],
        w_s, w_r,
    )
    gather_w.begin(0)
    gather_w.begin(1)
    sends.start(fin, fbuf.at[me.zh, me.y, pl.ds(4 * me.x, 4)], x_s.at[0], x_r.at[0], partner)

    for k in range(4):
        j = (me.y + k) % 4
        if k == 0:
            pltpu.make_async_copy(res.at[j], rbuf.at[me.y], e_r.at[0]).start()
        else:
            sends.start(res.at[j], rbuf.at[me.y], e_s.at[k], e_r.at[k], me.at(y=j))

    half = pl.ds(pl.multiple_of(me.c * 2048, 2048), 2048)
    other_half = pl.ds(pl.multiple_of(other_core * 2048, 2048), 2048)
    gather_w.level(0)
    for i in range(8):
        piece = cbuf.at[slot_of(me.zl), :, pl.ds(pl.multiple_of((me.c * 8 + i) * 256, 256), 256)]
        arrived(piece, a_r.at[i], sibling)

    base, pos = (me.zl // 4) * 4, me.zl % 4
    far = (me.zl + 4) % 8
    line = lambda zl: cbuf.at[slot_of(zl), :, half]
    sends.start(line(me.zl), line(me.zl), z_s.at[4], z_r.at[4], me.at(zl=far))
    for k in (1, 2, 3):
        sends.start(line(me.zl), line(me.zl), z_s.at[k], z_r.at[k], me.at(zl=base + (pos + k) % 4))
    sends.start(line(me.zl), line(me.zl), b_s.at[0], b_r.at[0], sibling)

    def from_z(k):
        zl = far if k == 4 else base + (pos - k) % 4 if k < 4 else (4 - base) + (pos - (k - 4)) % 4
        return zl

    def along_z(k):
        piece = line(from_z(k))
        arrived(piece, z_r.at[k], sibling)
        if k == 4:
            for i in (1, 2, 3):
                sends.start(piece, piece, z_s.at[4 + i], z_r.at[4 + i], me.at(zl=base + (pos + i) % 4))
        sends.start(piece, piece, b_s.at[k], b_r.at[k], sibling)

    gather_w.level(1)
    for k in (4, 1, 3, 2):
        along_z(k)
    gather_w.level(2)
    arrived(fbuf.at[1 - me.zh, me.y, pl.ds(4 * me.x, 4)], x_r.at[0], sibling)
    own_f.wait()
    fslot = lambda h, px, py: fbuf.at[(me.zh + h) % 2, py, pl.ds(4 * px, 4)]
    gather_f = Gather(me, sends, lambda h: fslot(h, me.x, me.y), fslot, f_s, f_r)
    gather_f.begin(0)
    gather_f.begin(1)
    for k in (5, 7, 6):
        along_z(k)
    for k in range(8):
        zl = me.zl if k == 0 else from_z(k)
        arrived(cbuf.at[slot_of(zl), :, other_half], b_r.at[k], sibling)
    own_w.wait()

    def project(sources):
        total = None
        for i, j in sources:
            px, py = gather_w.source(0, i, j)
            k = py * 4 + px
            a = cbuf[:, :, pl.ds(pl.multiple_of(k * 256, 256), 256)].reshape(128, 256)
            new = jnp.dot(a, wbuf[k], preferred_element_type=jnp.float32)
            total = new if total is None else total + new
        return total.reshape(8, 16, 512)

    gather_w.finish((0, 1), LAST[:4])
    part[...] = project(EARLY)
    gather_w.finish((0, 1), LAST[4:])
    part[...] += project(LATE)
    for k in range(4):
        arrived(rbuf.at[(me.y - k) % 4], e_r.at[k], sibling)
    mine = pl.ds(4 * me.zh, 4)
    part[mine] = part[mine] + rbuf[...].astype(jnp.float32)
    mine_out[...] = part[...].astype(jnp.bfloat16)
    for k in range(4):
        rows = pl.ds(2 * k, 2)
        sends.start(mine_out.at[rows], other.at[rows], x_s.at[1 + k], x_r.at[1 + k], partner)

    sslot = lambda k, px, py: sbuf.at[pl.ds(2 * k, 2), px * 4 + py]
    gather_s = Gather(me, sends, lambda k: sslot(k, me.x, me.y), sslot, s_s, s_r)

    def share(k):
        rows = pl.ds(2 * k, 2)
        arrived(other.at[rows], x_r.at[1 + k], sibling)
        new = (part[rows] + other[rows].astype(jnp.float32)).astype(jnp.bfloat16)
        sbuf[rows, me.n] = new

        @pl.when(feeds)
        def _():
            zbuf[me.zl // 2, rows] = new

        for v in (0, 2, 4, 6):

            @pl.when(spot == v)
            def _():
                for copy in line_copies(k, v, v):
                    copy.start()

        gather_s.begin(k)

    mirror = lambda v: v + me.zh * (7 - 2 * v)
    spot = mirror(me.zl)
    row_of = lambda source: source // 2 + me.zh * (3 - 2 * (source // 2))

    def line_copies(k, v, source):
        piece = zbuf.at[row_of(source), pl.ds(2 * k, 2)]
        return [
            pltpu.make_async_remote_copy(
                src_ref=piece, dst_ref=piece, send_sem=u_s.at[k * 16 + source * 2 + i], recv_sem=u_r.at[k * 4 + source // 2],
                device_id=me.at(zl=mirror(child)), device_id_type=MESH,
            )
            for i, child in enumerate(TREES[source].get(v, ()))
        ]

    def pass_along_z(k):
        for v in range(1, 8):

            @pl.when(spot == v)
            def _():
                for source in TREES:
                    if v != source and v in TREES[source]:
                        arrived(zbuf.at[row_of(source), pl.ds(2 * k, 2)], u_r.at[k * 4 + source // 2], sibling)
                        for copy in line_copies(k, v, source):
                            copy.start()

    def sent_along_z():
        for v in range(8):

            @pl.when(spot == v)
            def _():
                for k in range(4):
                    for source in TREES:
                        for copy in line_copies(k, v, source):
                            copy.wait_send()

    def swap(k, first):
        rows = pl.ds(2 * k, 2)
        for source in TREES:
            p = row_of(source)
            had = False
            for v in TREES[source]:
                had = had | (spot == v)
            who = had if first else jnp.logical_not(had)
            if not first:
                pl.when(who)(lambda: arrived(zbuf.at[p, rows], u_r.at[k * 4 + source // 2], sibling))
            for j in (0, 1):
                px = 2 * me.c + j
                here = (me.y == p) & (me.x == px)
                src, dst = zbuf.at[p, rows, :, pl.ds(256 * j, 256)], lbuf.at[rows, me.n]
                sends.start(
                    src, dst, t_s.at[k * 8 + source + j], t_r.at[k], me.at(y=p, x=px), cond=who & jnp.logical_not(here)
                )
                pl.when(who & here)(pltpu.make_async_copy(src, dst, t_r.at[k]).start)

    def to_sibling(k):
        piece = lbuf.at[pl.ds(2 * k, 2)]
        pl.when(on_line)(lambda: arrived(piece, t_r.at[k], sibling))
        sends.start(piece, piece, l_s.at[k], l_r.at[k], sibling, cond=on_line)

    def from_sibling(k):
        pl.when(jnp.logical_not(on_line))(lambda: arrived(lbuf.at[pl.ds(2 * k, 2)], l_r.at[k], sibling))

    def add(first, parts):
        rows = pl.ds(2 * first, 2 * parts)
        depth_of = parts * 512
        a = lbuf[rows].reshape(depth_of, 256)
        f = fbuf[first // 2, pl.ds(2 * (first % 2), 2 * parts)]
        dims = (((0,), (0,)), ((), ()))
        for out, buf in ((gram, sbuf[rows]), (cross, f)):
            new = lax.dot_general(a, buf.reshape(depth_of, 512), dims, preferred_element_type=jnp.float32) * (1.0 / 2048)
            out[...] = new if first == 0 else out[...] + new

    for slot in range(9):
        if slot == 0:
            gather_f.level(0)
            gather_f.level(1)
        if slot == 1:
            gather_f.level(2)
        if slot < 4:
            share(slot)
        for n in range(3):
            k = slot - 1 - n
            if 0 <= k < 4:
                gather_s.level(n, (k,))
        if 0 <= slot - 1 < 4:
            pass_along_z(slot - 1)
            swap(slot - 1, True)
        if 0 <= slot - 2 < 4:
            swap(slot - 2, False)
        if 0 <= slot - 5 < 4:
            to_sibling(slot - 5)
        if slot == 7:
            gather_f.finish()
            gather_s.finish((0, 1))
            from_sibling(0)
            from_sibling(1)
            add(0, 2)
    gather_s.finish((2,))
    from_sibling(2)
    add(2, 1)
    gather_s.finish((3,))
    from_sibling(3)
    add(3, 1)
    sent_along_z()
    sends.drain()


def body(context, out_weight, residual, final_states):
    vmem, hbm = pl.BlockSpec(memory_space=pltpu.VMEM), pl.BlockSpec(memory_space=pl.ANY)
    dma = lambda n: pltpu.SemaphoreType.DMA((n,))
    bf16, f32 = jnp.bfloat16, jnp.float32
    out = jax.ShapeDtypeStruct((256, 512), f32)
    return pl.pallas_call(
        kernel,
        out_shape=(out, out),
        in_specs=[hbm] * 4,
        out_specs=(vmem, vmem),
        scratch_shapes=[
            pltpu.VMEM((16, 256, 512), bf16),
            pltpu.VMEM((8, 16, 4096), bf16),
            pltpu.VMEM((4, 16, 512), bf16),
            pltpu.VMEM((8, 16, 512), f32),
            pltpu.VMEM((8, 16, 512), bf16),
            pltpu.VMEM((8, 16, 512), bf16),
            pltpu.VMEM((2, 4, 16, 16, 512), bf16),
            pltpu.VMEM((8, 16, 16, 512), bf16),
            pltpu.VMEM((4, 8, 16, 512), bf16),
            pltpu.VMEM((8, 16, 16, 256), bf16),
            dma(32), dma(32), dma(32), dma(32), dma(64), dma(64),
            dma(8), dma(8), dma(8), dma(8), dma(8), dma(8),
            dma(4), dma(4), dma(5), dma(5), dma(32), dma(4), dma(64), dma(16), dma(4), dma(4), dma(2),
        ],
        compiler_params=pltpu.CompilerParams(collective_id=0, has_side_effects=True, vmem_limit_bytes=56 << 20),
        cost_estimate=pl.CostEstimate(flops=1 << 31, bytes_accessed=1 << 21, transcendentals=0),
    )(context, out_weight, residual.reshape(4, 16, 512), final_states.reshape(4, 16, 512))


def solution(mesh):
    in_specs = (P("tensor", "dp"), P("dp", "tensor"), P("dp", "tensor"), P("dp", "tensor"))
    out_specs = (P("dp", "tensor"), P("dp", "tensor"))
    return jax.shard_map(body, mesh=mesh, in_specs=in_specs, out_specs=out_specs, check_vma=False)
```
